256 devices in a mesh: section: 8 (over x, core), tp: 32 (over y, z).
Axes of the slice: x: 4, y: 4, z: 8, core: 2. Of those that a mesh axis runs over, the one named last changes fastest.
Arguments:
- hidden: bfloat16 [2048, 8192], P(('section', 'tp')), may hold values from -6 to 6
- norm_gain: float32 [8, 8192], P('section'), may hold values from 0.5 to 1.5
- w_query: bfloat16 [8, 8192, 8192], P('section', None, 'tp'), may hold values from -0.125 to 0.125
- w_keyval: bfloat16 [8, 8192, 2048], P('section', None, 'tp'), may hold values from -0.0625 to 0.0625
- w_out: bfloat16 [8, 8192, 8192], P('section', 'tp'), may hold values from -0.25 to 0.25
- kv_pool: bfloat16 [8, 128, 128, 2048], P('section', 'tp'), may hold values from -70 to 70
- page_table: int32 [8, 128], P('section'), may hold values from 0 to 127, as said below
- prefix_len: int32 [8, 4], P('section'), may hold values from 1 to 4096, 10240 in all within a row
- decode_place: int32 [8, 32], P('section'), may hold values from 0 to 31, each once within a row
Outputs:
- handed: bfloat16 [2048, 8192], P(('section', 'tp'))
- decode_cache: bfloat16 [8, 32, 64, 256], P('section', 'tp')
The draws below stay inside these ranges and needn't reach their ends.
Inputs may be any that keep to these rules, and one draw needn't show every extreme that they name: `page_table`: every page of a section's pool appears once in its page table, and of the pages k * 4 to k * 4 + 3 exactly 1 stand in each request's list. `prefix_len`: some request of every section has exactly 4096 prefix tokens. `decode_place`: every slot appears once for each section.
All inputs are finite; a program needn't handle non-finite values.
Results may differ from the reference program's by a relative error of at most 0.024.
The reference program's roundings to bfloat16 on the way (of `normed`, `query`, `keyval`, `weights`, `attended` and `block`) count: a program that leaves them out, or rounds other values in their place, can miss the bound.
Values may be sent and summed in bfloat16 or wider, within the bound.
No kernel may reach another device: no remote copies, remote signals or barrier semaphores. Data moves between devices by JAX's collectives and lax.ppermute only.
A program may use at most 128 MiB of HBM per device.

```python
import math
import jax
import jax.numpy as jnp
import numpy as np
from jax import lax

D = 8192
H = 64
KVH = 8
HD = 128
PAGE = 128
REQ = 4
NEW = 64
POOL_DEV = 4
MAXPAGES = 32
TOTAL_ROWS = 2048
N_SECTION = 8
N_TP = 32


def draw_kv_pool(key, part):
    key = jax.random.fold_in(key, 11)
    shape = (N_SECTION, POOL_DEV * N_TP, PAGE, 2 * KVH * HD)
    first = jax.random.fold_in(key, 1)
    values = jnp.clip(jax.random.normal(first, shape, jnp.float32), -6.0, 6.0)
    return values.astype(jnp.bfloat16)


def draw_page_table(key, part):
    key = jax.random.fold_in(key, 23)
    per_request = POOL_DEV // REQ
    listed = POOL_DEV * N_TP // REQ

    def one_section(section_key):
        owner_key = jax.random.fold_in(section_key, 1)
        list_key = jax.random.fold_in(section_key, 2)
        local_order = jax.vmap(lambda k: jax.random.permutation(k, POOL_DEV))(jax.random.split(owner_key, N_TP))
        items = jax.vmap(lambda k: jax.random.permutation(k, listed))(jax.random.split(list_key, REQ))
        owners = items // per_request
        within = items % per_request
        request_ids = jnp.arange(REQ, dtype=jnp.int32)[:, None]
        local_page = local_order[owners, request_ids * per_request + within]
        return (owners * POOL_DEV + local_page).reshape(-1).astype(jnp.int32)
    return jax.vmap(one_section)(jax.random.split(key, N_SECTION))


def levels(stream_key, shape, cuts, smallest, high):
    level, own = 1.0, jax.random.fold_in(stream_key, 6)
    for position, parts in cuts:
        heights = jnp.exp(jax.random.uniform(jax.random.fold_in(own, position), (parts,), jnp.float32, smallest / len(cuts), high / len(cuts)))
        level = level * jnp.repeat(heights, shape[position] // parts).reshape([-1 if axis == position else 1 for axis in range(len(shape))])
    return level


def profile(count, total, bound, skew):
    weights = [(1 << 20) // math.isqrt(grade ** skew) + 1 for grade in range(2, count + 1)]
    surplus, given = total - bound - (count - 1), [1] * (count - 1)
    while surplus > 0:
        candidates = [i for i in range(count - 1) if given[i] < bound]
        mass, remaining = sum([weights[i] for i in candidates]), surplus
        for i in candidates:
            extra = min(bound - given[i], max(1, remaining * weights[i] // mass), surplus)
            given[i] = given[i] + extra
            surplus = surplus - extra
    return np.array([bound] + given)


def uneven(stream_key, number_of, total, limit, skew):
    if number_of == 2:
        one = jax.random.randint(stream_key, (), max(1, total - limit), min(limit, total - 1) + 1)
        return jnp.stack([one, total - one])
    lengths = jnp.asarray(profile(number_of, total, limit, skew), jnp.int32)
    pairs = (number_of - 1) // 2
    giver, receiver = lengths[1:1 + 2 * pairs:2], lengths[2:2 + 2 * pairs:2]
    room = jnp.minimum(giver - 1, limit - receiver)
    passed = jax.random.randint(jax.random.fold_in(stream_key, 1), (pairs,), 0, 1 << 20) % (room + 1)
    lengths = lengths.at[1:1 + 2 * pairs:2].set(giver - passed).at[2:2 + 2 * pairs:2].set(receiver + passed)
    return lengths[jax.random.permutation(jax.random.fold_in(stream_key, 2), number_of)]


def bell_draw(key, extent, scale, reach, cuts=(), kind=jnp.bfloat16):
    values = scale * jax.random.normal(key, extent, jnp.float32)
    if cuts:
        values = values * levels(key, extent, cuts, -0.22, 0.18)
    return jnp.clip(values, -reach, reach).astype(kind)


def setup_inputs(seed: int = 0) -> dict:
    key_of = jax.random.split(jax.random.key(seed), 10)
    return {
        "hidden": bell_draw(key_of[0], (TOTAL_ROWS, D), 1.0, 6.0, ((0, 256),)),
        "norm_gain": jnp.clip(1.0 + 0.1 * jax.random.normal(key_of[1], (N_SECTION, D), jnp.float32), 0.5, 1.5),
        "w_query": bell_draw(key_of[2], (N_SECTION, D, H * HD), (D // 4) ** -0.5, 0.125, ((0, 8), (2, 32))),
        "w_keyval": bell_draw(key_of[3], (N_SECTION, D, 2 * KVH * HD), D ** -0.5, 0.0625, ((0, 8), (2, 32))),
        "w_out": bell_draw(key_of[4], (N_SECTION, H * HD, D), (H * HD // 16) ** -0.5, 0.25, ((0, 8), (1, 32))),
        "kv_pool": draw_kv_pool(jax.random.fold_in(key_of[9], 71), 0),
        "page_table": draw_page_table(jax.random.fold_in(key_of[9], 71), 0),
        "prefix_len": jax.vmap(lambda own: uneven(own, REQ, REQ * MAXPAGES * PAGE * 5 // 8, MAXPAGES * PAGE, 2))(jax.random.split(key_of[7], N_SECTION)).reshape((N_SECTION, REQ)).astype(jnp.int32),
        "decode_place": jax.vmap(lambda own: jax.random.permutation(own, REQ * KVH))(jax.random.split(key_of[8], N_SECTION)).reshape((N_SECTION, REQ * KVH)).astype(jnp.int32),
    }


rope_theta = 500000.0

def rotate(values, positions, dims, apply, head_size):
    rows = values.shape[0]
    cols = values.shape[1]
    inverse = jnp.power(rope_theta, -(dims // 2 * 2).astype(jnp.float32) / head_size)
    angle = positions[:, None].astype(jnp.float32) * inverse[None, :]
    cosine = jnp.cos(angle)[:, 0::2]
    sine = jnp.sin(angle)[:, 0::2]
    pairs = values.reshape(rows, cols // 2, 2)
    even = pairs[:, :, 0]
    odd = pairs[:, :, 1]
    turned = jnp.stack([even * cosine - odd * sine, even * sine + odd * cosine], axis=-1).reshape(rows, cols)
    return jnp.where(apply[None, :], turned, values)

def layer(rows_in, gain, wq, wkv, wo, pool, table, lens, place):
    maxpages = table.shape[0] // REQ
    prefix = maxpages * PAGE
    group = H // KVH
    xf = rows_in.astype(jnp.float32)
    meansq = lax.optimization_barrier(jnp.mean(xf * xf, axis=-1, keepdims=True))
    normed = (xf * lax.rsqrt(meansq + 1e-05) * gain[None, :]).astype(jnp.bfloat16)
    query_raw = jnp.dot(normed, wq, preferred_element_type=jnp.float32)
    keyval_raw = jnp.dot(normed, wkv, preferred_element_type=jnp.float32)
    positions = (lens[:, None] + jnp.arange(NEW, dtype=jnp.int32)[None, :]).reshape(-1)
    qcols = jnp.arange(H * HD, dtype=jnp.int32)
    query = rotate(query_raw, positions, qcols % HD, qcols >= 0, HD).astype(jnp.bfloat16)
    kcols = jnp.arange(2 * KVH * HD, dtype=jnp.int32)
    keyval = rotate(keyval_raw, positions, kcols % HD, kcols // HD % 2 == 0, HD).astype(jnp.bfloat16)
    pages = pool[table.reshape(REQ, maxpages)].reshape(REQ, prefix, KVH, 2 * HD)
    fresh = keyval.reshape(REQ, NEW, KVH, 2 * HD)
    keys = jnp.concatenate([pages, fresh], axis=1)
    kpos = jnp.arange(prefix + NEW, dtype=jnp.int32)
    npos = jnp.arange(NEW, dtype=jnp.int32)
    visible = jnp.where(kpos[None, None, :] < prefix, kpos[None, None, :] < lens[:, None, None], kpos[None, None, :] - prefix <= npos[None, :, None])
    visible = visible[:, None, :, :]
    qheads = query.reshape(REQ, NEW, KVH, group, HD).transpose(2, 0, 1, 3, 4)
    kheads = keys.transpose(2, 0, 1, 3)

    def one_head(pair):
        qh, kh = pair
        scores = jnp.einsum('rngd,rkd->rgnk', qh.astype(jnp.float32), kh[:, :, :HD].astype(jnp.float32)) * HD ** (-0.5)
        top = lax.optimization_barrier(jnp.max(jnp.where(visible, scores, -1e+30), axis=-1, keepdims=True))
        expo = jnp.where(visible, jnp.exp(scores - top), 0.0)
        weights = (expo / lax.optimization_barrier(jnp.sum(expo, axis=-1, keepdims=True))).astype(jnp.bfloat16)
        return jnp.einsum('rgnk,rkd->rngd', weights.astype(jnp.float32), kh[:, :, HD:].astype(jnp.float32)).astype(jnp.bfloat16)
    heads_out = lax.map(one_head, (qheads, kheads))
    attended = heads_out.transpose(1, 2, 0, 3, 4).reshape(REQ * NEW, H * HD)
    block = (xf + jnp.dot(attended, wo, preferred_element_type=jnp.float32)).astype(jnp.bfloat16)
    units = fresh.transpose(0, 2, 1, 3).reshape(REQ * KVH, NEW, 2 * HD)
    cache = jnp.zeros((REQ * KVH, NEW, 2 * HD), jnp.bfloat16).at[place].set(units)
    return (block, cache)

def reference(hidden, norm_gain, w_query, w_keyval, w_out, kv_pool, page_table, prefix_len, decode_place):
    rows = REQ * NEW
    blocks = []
    caches = []
    for section in range(N_SECTION):
        block, cache = layer(hidden[section * rows:(section + 1) * rows], norm_gain[section], w_query[section], w_keyval[section], w_out[section], kv_pool[section], page_table[section], prefix_len[section], decode_place[section])
        blocks.append(block)
        caches.append(cache)
    stacked = jnp.stack(blocks, axis=0)
    handed = jnp.roll(stacked, 1, axis=0).reshape(N_SECTION * rows, D)
    return (handed, jnp.stack(caches, axis=0))
```

```python
import functools

import jax
import jax.numpy as jnp
from jax import lax
from jax.experimental import pallas as pl
from jax.experimental.pallas import tpu as pltpu
from jax.sharding import Mesh, PartitionSpec as P

D = 8192
KVH = 8
HD = 128
PAGE = 128
REQ = 4
NEW = 64
NY = 4
NZ = 8
NTP = 32
QC = 256
GROUP = 8

rope_theta = 500000.0
f32 = jnp.float32
bf16 = jnp.bfloat16
VMEM_LIMIT = 60 * 1024 * 1024


def shift(value, axis, steps):
    count = lax.axis_size(axis)
    return lax.ppermute(value, axis, [(i, (i + steps) % count) for i in range(count)])


def shift_quad(value, steps):
    pairs = [(q * 4 + i, q * 4 + (i + steps) % 4) for q in range(2) for i in range(4)]
    return lax.ppermute(value, "z", pairs)


def regroup_kernel(order_ref, place_ref, pool_ref, *outs):
    for k, out in enumerate(outs):
        first = lax.rem(place_ref[0] + k, NY) * (4 * HD)
        for h in range(2):
            at = pl.multiple_of(first + h * 2 * HD, 2 * HD)
            out[h, 0] = pool_ref[0, :, pl.ds(at, 2 * HD)]


def regroup(pool, order, place):
    out = pl.BlockSpec((2, 1, PAGE, 2 * HD), lambda r, order, place: (0, r, 0, 0))
    return pl.pallas_call(
        regroup_kernel,
        grid_spec=pltpu.PrefetchScalarGridSpec(
            num_scalar_prefetch=2,
            grid=(REQ,),
            in_specs=[
                pl.BlockSpec((1, PAGE, 2 * KVH * HD), lambda r, order, place: (order[r], 0, 0))
            ],
            out_specs=[out] * NY,
        ),
        out_shape=[jax.ShapeDtypeStruct((2, REQ, PAGE, 2 * HD), bf16)] * NY,
    )(order, place, pool)


Z_ORDER = (0, -1, 1, -2, 2, -3, 3, -4)
Y_ORDER = (0, -1, 1, -2)


def project_kernel(
    place_ref,
    x0,
    x1,
    x2,
    x3a,
    x3b,
    wq,
    wkv,
    cosine,
    sine,
    cosine_kv,
    sine_kv,
    o0,
    o1,
    o2,
    o3,
    acc,
    turned,
    ready,
):
    step = pl.program_id(0)
    rows = jnp.concatenate([x0[...], x1[...], x2[...], x3a[...], x3b[...]], axis=0)
    part_q = jnp.dot(rows, wq[...], preferred_element_type=f32)
    part_kv = jnp.dot(rows, wkv[...], preferred_element_type=f32)

    @pl.when(step == 0)
    def _():
        acc[:, :QC] = part_q
        acc[:, QC:] = part_kv

    @pl.when(step > 0)
    def _():
        acc[:, :QC] += part_q
        acc[:, QC:] += part_kv

    @pl.when(step == pl.num_programs(0) - 1)
    def _():
        for k in range(NY):
            for j in range(NZ):
                yk = lax.rem(place_ref[0] + (Y_ORDER[k] + NY), NY)
                zj = lax.rem(place_ref[1] + (Z_ORDER[j] + NZ), NZ)
                at = pl.multiple_of(yk * 64 + zj * 8, 8)
                turned[pl.ds(at, 8), :] = acc[k * 64 + j * 8 : k * 64 + j * 8 + 8, :]
        even = lax.broadcasted_iota(jnp.int32, (REQ * NEW, HD), 1) % 2 == 0
        for c in range(3):
            v = turned[:, c * HD : (c + 1) * HD]
            cs, sn = (cosine, sine) if c < 2 else (cosine_kv, sine_kv)
            other = jnp.where(even, -pltpu.roll(v, HD - 1, 1), pltpu.roll(v, 1, 1))
            done = (v * cs[...] + other * sn[...]).astype(bf16)
            for r in range(REQ):
                ready[r, :, c * HD : (c + 1) * HD] = done[r * NEW : (r + 1) * NEW]
        for k, out in enumerate((o0, o1, o2, o3)):
            out[...] = ready[lax.rem(place_ref[2] + k, REQ)]


def project(place, pieces, wq, wkv, tables):
    kc = 1024
    rows = [p.shape[0] for p in pieces]
    whole = pl.BlockSpec((REQ * NEW, HD), lambda k, p: (0, 0))
    return pl.pallas_call(
        project_kernel,
        grid_spec=pltpu.PrefetchScalarGridSpec(
            num_scalar_prefetch=1,
            grid=(D // kc,),
            in_specs=[pl.BlockSpec((r, kc), lambda k, p: (0, k)) for r in rows]
            + [
                pl.BlockSpec((kc, QC), lambda k, p: (k, 0)),
                pl.BlockSpec((kc, HD), lambda k, p: (k, 0)),
            ]
            + [whole] * 4,
            out_specs=[pl.BlockSpec((NEW, QC + HD), lambda k, p: (0, 0))] * REQ,
            scratch_shapes=[
                pltpu.VMEM((REQ * NEW, QC + HD), f32),
                pltpu.VMEM((REQ * NEW, QC + HD), f32),
                pltpu.VMEM((REQ, NEW, QC + HD), bf16),
            ],
        ),
        out_shape=[jax.ShapeDtypeStruct((NEW, QC + HD), bf16)] * REQ,
        compiler_params=pltpu.CompilerParams(vmem_limit_bytes=VMEM_LIMIT),
    )(place, *pieces, wq, wkv, *tables)


CARRY = NEW * 2 * HD // 8


CHUNK = 4


def attend_kernel(info_ref, p0, p1, p2, p3, kv_ref, o0, o1, o2, o3, unit_ref, q_s, s_s, fresh):
    pieces = (p0, p1, p2, p3)
    member = info_ref[0]
    length = info_ref[1]
    for k in range(4):
        for h in range(2):
            row = (k * 2 + h) * NEW
            q_s[row : row + NEW, :] = pieces[k][:, h * HD : (h + 1) * HD]
        fresh[k] = pieces[k][:, QC:].astype(f32)
    key_new = fresh[lax.rem(member, 4)] + fresh[lax.rem(member + 3, 4)]
    val_new = fresh[lax.rem(member + 2, 4)] + fresh[lax.rem(member + 1, 4)]
    for a in range(8):
        at = a * 2 * HD
        rows = slice(a * 8, a * 8 + 8)
        unit_ref[:, at : at + HD] = key_new[rows].astype(bf16)
        unit_ref[:, at + HD : at + 2 * HD] = val_new[rows].astype(bf16)
    key_new, val_new = key_new.astype(bf16), val_new.astype(bf16)
    q = q_s[...]
    rows = GROUP * NEW
    nt = (((1,), (1,)), ((), ()))
    s_new = lax.dot_general(q, key_new, nt, preferred_element_type=f32)
    token = lax.broadcasted_iota(jnp.int32, (rows, NEW), 0) % NEW
    s_new = jnp.where(lax.broadcasted_iota(jnp.int32, (rows, NEW), 1) <= token, s_new, -1e30)
    top = jnp.full((rows, HD), -1e30, f32)
    lane = lax.broadcasted_iota(jnp.int32, (1, HD), 1)
    width = CHUNK * PAGE
    for c in range(NTP // CHUNK):
        keys = kv_ref[c * CHUNK : (c + 1) * CHUNK, :, :HD].reshape(width, HD)
        s = lax.dot_general(q, keys, nt, preferred_element_type=f32)
        for o in range(CHUNK):
            start = info_ref[2 + c * CHUNK + o] * PAGE
            part = jnp.where(lane < length - start, s[:, o * PAGE : (o + 1) * PAGE], -1e30)
            s_s[:, c * width + o * PAGE : c * width + (o + 1) * PAGE] = part
            top = jnp.maximum(top, part)
    m = jnp.maximum(
        jnp.max(top, axis=1, keepdims=True), jnp.max(s_new, axis=1, keepdims=True)
    )
    factor = HD ** (-0.5) * 1.4426950408889634
    e_new = jnp.exp2((s_new - m) * factor)
    total = jnp.zeros((rows, HD), f32)
    for c in range(NTP):
        e = jnp.exp2((s_s[:, c * PAGE : (c + 1) * PAGE] - m) * factor)
        s_s[:, c * PAGE : (c + 1) * PAGE] = e
        total = total + e
    inverse = 1.0 / (
        jnp.sum(total, axis=1, keepdims=True) + jnp.sum(e_new, axis=1, keepdims=True)
    )
    mixed = jnp.dot((e_new * inverse).astype(bf16), val_new, preferred_element_type=f32)
    for c in range(NTP // CHUNK):
        vals = kv_ref[c * CHUNK : (c + 1) * CHUNK, :, HD:].reshape(width, HD)
        w = (s_s[:, c * width : (c + 1) * width] * inverse).astype(bf16)
        mixed = mixed + jnp.dot(w, vals, preferred_element_type=f32)
    mixed = mixed.astype(bf16)
    for k, out in enumerate((o0, o1, o2, o3)):
        for h in range(2):
            row = (k * 2 + h) * NEW
            out[:, h * HD : (h + 1) * HD] = mixed[row : row + NEW]


def attend(info, pieces, kv):
    vm = pl.BlockSpec(memory_space=pltpu.VMEM)
    return pl.pallas_call(
        attend_kernel,
        in_specs=[pl.BlockSpec(memory_space=pltpu.SMEM)] + [vm] * 5,
        out_specs=[vm] * 5,
        out_shape=[jax.ShapeDtypeStruct((NEW, QC), bf16)] * 4
        + [jax.ShapeDtypeStruct((8, CARRY), bf16)],
        scratch_shapes=[
            pltpu.VMEM((GROUP * NEW, HD), bf16),
            pltpu.VMEM((GROUP * NEW, NTP * PAGE), f32),
            pltpu.VMEM((4, NEW, HD), f32),
        ],
        compiler_params=pltpu.CompilerParams(vmem_limit_bytes=VMEM_LIMIT),
    )(info, *pieces, kv)


OUT_COLS = 2048


def outward_kernel(place_ref, a0, a1, a2, a3, wo, o0, o1, o2, o3, rows):
    @pl.when(pl.program_id(0) == 0)
    def _():
        for k, piece in enumerate((a0, a1, a2, a3)):
            at = lax.rem(place_ref[2] + k + 4 - place_ref[0], 4)
            rows[pl.ds(pl.multiple_of(at * NEW, NEW), NEW), :] = piece[...]

    part = jnp.dot(rows[...], wo[...], preferred_element_type=f32).astype(bf16)
    for j, out in enumerate((o0, o1, o2, o3)):
        out[...] = part[j * NEW : (j + 1) * NEW]


def outward(place, pieces, wo, first, cols):
    steps = cols // OUT_COLS
    lead = first // OUT_COLS
    return pl.pallas_call(
        outward_kernel,
        grid_spec=pltpu.PrefetchScalarGridSpec(
            num_scalar_prefetch=1,
            grid=(steps,),
            in_specs=[pl.BlockSpec((NEW, QC), lambda n, p: (0, 0))] * 4
            + [pl.BlockSpec((QC, OUT_COLS), lambda n, p: (0, n + lead))],
            out_specs=[pl.BlockSpec((NEW, OUT_COLS), lambda n, p: (0, n))] * 4,
            scratch_shapes=[pltpu.VMEM((REQ * NEW, QC), bf16)],
        ),
        out_shape=[jax.ShapeDtypeStruct((NEW, cols), bf16)] * 4,
        compiler_params=pltpu.CompilerParams(vmem_limit_bytes=VMEM_LIMIT),
    )(place, *pieces, wo)


def gather_kernel(pick_ref, b0, b1, b2, *rest):
    total = b0[...].astype(f32) + b1[...].astype(f32) + b2[...].astype(f32)
    cols = total.shape[1]
    out_ref = rest[NY] if len(rest) > 1 else rest[0]
    for k in range(NZ):
        out_ref[k, :, :cols] = total[k * 8 : k * 8 + 8].astype(bf16)
    if len(rest) > 1:
        units = rest[NY + 1]
        for k in range(NY):
            units[k] = rest[k][...]
        for k in range(NZ):
            out_ref[k, :, cols:] = units[pick_ref[k]]


def gather_blocks(pick, blocks, units):
    cols = blocks[0].shape[1] + (CARRY if units else 0)
    vm = pl.BlockSpec(memory_space=pltpu.VMEM)
    return pl.pallas_call(
        gather_kernel,
        in_specs=[pl.BlockSpec(memory_space=pltpu.SMEM)] + [vm] * (3 + len(units)),
        out_specs=vm,
        out_shape=jax.ShapeDtypeStruct((NZ, 8, cols), bf16),
        scratch_shapes=[pltpu.VMEM((NY, 8, CARRY), bf16)] if units else [],
        compiler_params=pltpu.CompilerParams(vmem_limit_bytes=VMEM_LIMIT),
    )(pick, *blocks, *units)


def sum_over_y(blocks):
    half = blocks[2].shape[1] // 2
    right = shift(blocks[2][:, :half], "y", 1)
    left = shift(blocks[2][:, half:], "y", -1)
    none = jnp.zeros((NEW, half), f32)
    to_right = blocks[1].astype(f32) + jnp.concatenate([right.astype(f32), none], axis=1)
    to_left = blocks[3].astype(f32) + jnp.concatenate([none, left.astype(f32)], axis=1)
    return (
        blocks[0],
        shift(to_right.astype(bf16), "y", 1),
        shift(to_left.astype(bf16), "y", -1),
    )


def to_next(value):
    return shift(value, "section", 1)


def local(
    hidden, norm_gain, w_query, w_keyval, w_out, kv_pool, page_table, prefix_len, decode_place
):
    y = lax.axis_index("y")
    z = lax.axis_index("z")
    rank = y * NZ + z
    member = rank % 4
    place = jnp.stack([y, z, member]).astype(jnp.int32)
    lens = prefix_len[0]
    table = page_table[0].reshape(REQ, -1)

    order = jnp.sum(jnp.where(table // 4 == rank, table % 4, 0), axis=1).astype(jnp.int32)
    toward = [t.reshape(NZ, PAGE, 2 * HD) for t in regroup(kv_pool[0], order, place)]
    column = [toward[0]] + [shift(toward[k], "y", k) for k in range(1, NY)]

    xf = hidden.astype(f32)
    meansq = jnp.mean(xf * xf, axis=-1, keepdims=True)
    normed = (xf * lax.rsqrt(meansq + 1e-05) * norm_gain[0][None, :]).astype(bf16)
    half = D // 2
    r1, l1 = shift(normed, "z", 1), shift(normed, "z", -1)
    r2, l2 = shift(r1, "z", 1), shift(l1, "z", -1)
    r3, l3 = shift(r2, "z", 1), shift(l2, "z", -1)
    r4, l4 = shift(r3[:, :half], "z", 1), shift(l3[:, half:], "z", -1)
    mine = jnp.concatenate([normed, r1, l1, r2, l2, r3, l3, jnp.concatenate([r4, l4], 1)], 0)
    *column, mine = lax.optimization_barrier((*column, mine))
    kv = lax.all_to_all(jnp.stack(column, axis=1), "z", split_axis=0, concat_axis=0, tiled=True)
    kv = kv.reshape(NTP, PAGE, 2 * HD)
    yr1, yl1 = shift(mine, "y", 1), shift(mine, "y", -1)
    yr2, yl2 = shift(yr1[:32], "y", 1), shift(yl1[32:], "y", -1)

    dims = jnp.arange(HD, dtype=jnp.int32)
    positions = (lens[:, None] + jnp.arange(NEW, dtype=jnp.int32)[None, :]).reshape(-1)
    inverse = jnp.power(rope_theta, -(dims // 2 * 2).astype(f32) / HD)
    angle = positions[:, None].astype(f32) * inverse[None, :]
    cosine, sine = jnp.cos(angle), jnp.sin(angle)
    is_key = member < 2
    tables = (cosine, sine, jnp.where(is_key, cosine, 1.0), jnp.where(is_key, sine, 0.0))
    wkv = w_keyval[0]
    zero = jnp.zeros_like(wkv)
    odd = member % 2 == 1
    wkv = jnp.concatenate([jnp.where(odd, zero, wkv), jnp.where(odd, wkv, zero)], axis=1)
    projected = project(place, (mine, yr1, yl1, yr2, yl2), w_query[0], wkv, tables)

    got = [projected[0]] + [shift_quad(projected[k], k) for k in (1, 2, 3)]
    my_table = lax.dynamic_index_in_dim(table, member, 0, keepdims=False)
    owners = jnp.arange(NTP, dtype=jnp.int32)
    owners = (y - owners % NY) % NY * NZ + owners // NY
    starts = jnp.sum(
        jnp.where(my_table[None, :] // 4 == owners[:, None], jnp.arange(NTP)[None, :], 0), axis=1
    )
    my_len = jnp.sum(jnp.where(jnp.arange(REQ) == member, lens, 0))
    info = jnp.concatenate([jnp.stack([member, my_len]), starts]).astype(jnp.int32)
    *attended, unit = attend(info, got, kv)
    back = [attended[0]] + [shift_quad(attended[k], -k) for k in (1, 2, 3)]

    places = decode_place[0]
    slots = y * NZ + jnp.arange(NZ, dtype=jnp.int32)
    unit_ids = jnp.arange(REQ * KVH, dtype=jnp.int32)
    held = jnp.sum(jnp.where(places[None, :] == slots[:, None], unit_ids[None, :], 0), axis=1)
    holder = held % KVH * 4 + held // KVH
    pick = (y - holder // NZ) % NY
    units = [unit] + [shift(unit, "y", k) for k in (1, 2, 3)]

    parts = []
    for first in range(0, D, D // 2):
        blocks = outward(place, back, w_out[0], first, D // 2)
        sums = gather_blocks(pick.astype(jnp.int32), sum_over_y(blocks), units)
        units = []
        parts.append(lax.all_to_all(sums, "z", split_axis=0, concat_axis=0, tiled=True))
    summed = jnp.concatenate(
        [jnp.sum(p[:, :, : D // 2].astype(f32), axis=0) for p in parts], axis=1
    )
    handed = to_next((xf + summed).astype(bf16))
    wanted = jnp.sum(jnp.where(places == rank, unit_ids, 0))
    from_z = (wanted % KVH * 4 + wanted // KVH) % NZ
    decode_cache = lax.dynamic_index_in_dim(parts[0][:, :, D // 2 :], from_z, 0, keepdims=False)
    decode_cache = decode_cache.reshape(8, 8, 2 * HD).transpose(1, 0, 2)
    return handed, decode_cache.reshape(1, 1, NEW, 2 * HD)


def solution(mesh):
    names = ("section", "y", "z")
    tp = ("y", "z")
    grid = Mesh(mesh.devices.reshape(mesh.devices.shape[0], NY, NZ), names)
    placed = (
        P(names, None),
        P("section", None),
        P("section", None, tp),
        P("section", None, tp),
        P("section", tp, None),
        P("section", tp, None, None),
        P("section", None),
        P("section", None),
        P("section", None),
    )
    return jax.shard_map(
        local,
        mesh=grid,
        in_specs=placed,
        out_specs=(P(names, None), P("section", tp, None, None)),
        check_vma=False,
    )
```

```python
import functools

import jax
import jax.numpy as jnp
from jax import lax
from jax.experimental import pallas as pl
from jax.experimental.pallas import tpu as pltpu
from jax.sharding import Mesh, PartitionSpec as P

D = 8192
KVH = 8
HD = 128
PAGE = 128
REQ = 4
NEW = 64
NY = 4
NZ = 8
NTP = 32
QC = 256
GROUP = 8

rope_theta = 500000.0
f32 = jnp.float32
bf16 = jnp.bfloat16
MIB = 1024 * 1024


def takes(us):
    return pl.CostEstimate(flops=0, bytes_accessed=int(us * 3.3e6), transcendentals=0)


def shift(value, axis, steps):
    count = lax.axis_size(axis)
    return lax.ppermute(value, axis, [(i, (i + steps) % count) for i in range(count)])


def shift_quad(value, steps):
    pairs = [(q * 4 + i, q * 4 + (i + steps) % 4) for q in range(2) for i in range(4)]
    return lax.ppermute(value, "z", pairs)


def regroup_kernel(table_ref, pool_ref, *outs):
    y = lax.axis_index("y")
    rank = y * NZ + lax.axis_index("z")
    for r in range(REQ):
        page = jnp.int32(0)
        for j in range(NTP):
            entry = table_ref[r * NTP + j]
            page = jnp.where(lax.shift_right_logical(entry, 2) == rank, entry & 3, page)
        for k, out in enumerate(outs):
            first = lax.rem(y + k, NY) * (4 * HD)
            for h in range(2):
                at = pl.multiple_of(first + h * 2 * HD, 2 * HD)
                out[h, r] = pool_ref[page, :, pl.ds(at, 2 * HD)]


def regroup(table, pool):
    vm = pl.BlockSpec(memory_space=pltpu.VMEM)
    return pl.pallas_call(
        regroup_kernel,
        in_specs=[pl.BlockSpec(memory_space=pltpu.SMEM), vm],
        out_specs=[vm] * NY,
        out_shape=[jax.ShapeDtypeStruct((2, REQ, PAGE, 2 * HD), bf16)] * NY,
        cost_estimate=takes(2),
        compiler_params=pltpu.CompilerParams(vmem_limit_bytes=16 * MIB),
    )(table, pool)


def by_z_kernel(c0, c1, c2, c3, out):
    for z in range(NZ):
        for k, column in enumerate((c0, c1, c2, c3)):
            out[z, k] = column[z]


def by_z(column):
    vm = pl.BlockSpec(memory_space=pltpu.VMEM)
    return pl.pallas_call(
        by_z_kernel,
        in_specs=[vm] * NY,
        out_specs=vm,
        out_shape=jax.ShapeDtypeStruct((NZ, NY, PAGE, 2 * HD), bf16),
        cost_estimate=takes(2),
        compiler_params=pltpu.CompilerParams(vmem_limit_bytes=16 * MIB),
    )(*column)


Z_ORDER = (0, -1, 1, -2, 2, -3, 3, -4)
KC = 2048


def project_kernel(ks, split, last, *refs):
    place_ref, refs = refs[0], refs[1:]
    pieces, refs = refs[: len(split)], refs[len(split) :]
    wq, wkv, cosine, sine, cosine_kv, sine_kv = refs[:6]
    before, refs = refs[6 : 6 + 2 * last], refs[6 + 2 * last :]
    outs, (acc, turned, wide, *ready) = refs[: -3 - last], refs[-3 - last :]
    step = pl.program_id(0)
    mine = lax.rem(place_ref[2], 2) * 64
    wide[pl.ds(pl.multiple_of(mine, 64), 64), :] = wkv[...]
    wide[pl.ds(pl.multiple_of(64 - mine, 64), 64), :] = jnp.zeros((64, KC), bf16)
    rows = jnp.concatenate([piece[...] for piece in pieces], axis=0)
    part_q = jnp.dot(rows, wq[...], preferred_element_type=f32)
    part_kv = lax.dot_general(
        rows, wide[...], (((1,), (1,)), ((), ())), preferred_element_type=f32
    )

    @pl.when(step == 0)
    def _():
        acc[:, :QC] = part_q
        acc[:, QC:] = part_kv

    @pl.when(step > 0)
    def _():
        acc[:, :QC] += part_q
        acc[:, QC:] += part_kv

    @pl.when(step == pl.num_programs(0) - 1)
    def _():
        even = lax.broadcasted_iota(jnp.int32, (NEW, HD), 1) % 2 == 0
        for n, k in enumerate(ks):
            request = lax.rem(place_ref[0] + (k + NY), NY)
            for j in range(NZ):
                zj = lax.rem(place_ref[1] + (Z_ORDER[j] + NZ), NZ)
                turned[pl.ds(pl.multiple_of(zj * 8, 8), 8), :] = acc[
                    n * NEW + j * 8 : n * NEW + j * 8 + 8, :
                ]
            for c in range(3):
                v = turned[:, c * HD : (c + 1) * HD]
                cs, sn = (cosine, sine) if c < 2 else (cosine_kv, sine_kv)
                other = jnp.where(even, -pltpu.roll(v, HD - 1, 1), pltpu.roll(v, 1, 1))
                done = (v * cs[request] + other * sn[request]).astype(bf16)
                if last:
                    ready[0][request, :, c * HD : (c + 1) * HD] = done
                else:
                    outs[0][n, :, c * HD : (c + 1) * HD] = done
        if last:
            for n, k in enumerate((0, -1, 1)):
                request = lax.rem(place_ref[0] + (k + NY), NY)
                ready[0][request] = before[0][0] if n == 0 else before[1][n - 1]
            for k, out in enumerate(outs):
                out[...] = ready[0][lax.rem(place_ref[2] + k, REQ)]


def project(place, pieces, ks, wq, wkv, tables, before=()):
    split = [p.shape[0] for p in pieces]
    last = 1 if before else 0
    rows = sum(split)
    whole = pl.BlockSpec((REQ, NEW, HD), lambda k, p: (0, 0, 0))
    width = QC + HD
    if last:
        out_specs = [pl.BlockSpec((NEW, width), lambda k, p: (0, 0))] * REQ
        out_shape = [jax.ShapeDtypeStruct((NEW, width), bf16)] * REQ
    else:
        out_specs = [pl.BlockSpec((len(ks), NEW, width), lambda k, p: (0, 0, 0))]
        out_shape = [jax.ShapeDtypeStruct((len(ks), NEW, width), bf16)]
    out = pl.pallas_call(
        functools.partial(project_kernel, ks, split, last),
        grid_spec=pltpu.PrefetchScalarGridSpec(
            num_scalar_prefetch=1,
            grid=(D // KC,),
            in_specs=[pl.BlockSpec((r, KC), lambda k, p: (0, k)) for r in split]
            + [
                pl.BlockSpec((KC, QC), lambda k, p: (k, 0)),
                pl.BlockSpec((64, KC), lambda k, p: (0, k)),
            ]
            + [whole] * 4
            + [pl.BlockSpec(b.shape, lambda k, p: (0, 0, 0)) for b in before],
            out_specs=out_specs,
            scratch_shapes=[
                pltpu.VMEM((rows, width), f32),
                pltpu.VMEM((NEW, width), f32),
                pltpu.VMEM((HD, KC), bf16),
            ]
            + [pltpu.VMEM((REQ, NEW, width), bf16)] * last,
        ),
        out_shape=out_shape,
        cost_estimate=takes(5),
        compiler_params=pltpu.CompilerParams(vmem_limit_bytes=16 * MIB),
    )(place, *pieces, wq, wkv, *tables, *before)
    return out if last else out[0]


CHUNK = 4


def attend_kernel(info_ref, p0, p1, p2, p3, kv_ref, o0, o1, o2, o3, q_s, s_s, fresh):
    pieces = (p0, p1, p2, p3)
    member = info_ref[0]
    length = info_ref[1]
    for k in range(4):
        for h in range(2):
            row = (k * 2 + h) * NEW
            q_s[row : row + NEW, :] = pieces[k][:, h * HD : (h + 1) * HD]
        fresh[k] = pieces[k][:, QC:].astype(f32)
    key_new = (fresh[lax.rem(member, 4)] + fresh[lax.rem(member + 3, 4)]).astype(bf16)
    val_new = (fresh[lax.rem(member + 2, 4)] + fresh[lax.rem(member + 1, 4)]).astype(bf16)
    for out in (o0, o1, o2, o3):
        out[:, QC : QC + HD] = key_new
        out[:, QC + HD :] = val_new
    q = q_s[...]
    rows = GROUP * NEW
    nt = (((1,), (1,)), ((), ()))
    s_new = lax.dot_general(q, key_new, nt, preferred_element_type=f32)
    token = lax.broadcasted_iota(jnp.int32, (rows, NEW), 0) % NEW
    s_new = jnp.where(lax.broadcasted_iota(jnp.int32, (rows, NEW), 1) <= token, s_new, -1e30)
    top = jnp.full((rows, HD), -1e30, f32)
    lane = lax.broadcasted_iota(jnp.int32, (1, HD), 1)
    width = CHUNK * PAGE
    for c in range(NTP // CHUNK):
        keys = kv_ref[c * CHUNK : (c + 1) * CHUNK, :, :HD].reshape(width, HD)
        s = lax.dot_general(q, keys, nt, preferred_element_type=f32)
        for o in range(CHUNK):
            start = info_ref[2 + c * CHUNK + o] * PAGE
            part = jnp.where(lane < length - start, s[:, o * PAGE : (o + 1) * PAGE], -1e30)
            s_s[:, c * width + o * PAGE : c * width + (o + 1) * PAGE] = part
            top = jnp.maximum(top, part)
    m = jnp.maximum(
        jnp.max(top, axis=1, keepdims=True), jnp.max(s_new, axis=1, keepdims=True)
    )
    factor = HD ** (-0.5) * 1.4426950408889634
    e_new = jnp.exp2((s_new - m) * factor)
    total = jnp.zeros((rows, HD), f32)
    for c in range(NTP):
        e = jnp.exp2((s_s[:, c * PAGE : (c + 1) * PAGE] - m) * factor)
        s_s[:, c * PAGE : (c + 1) * PAGE] = e
        total = total + e
    inverse = 1.0 / (
        jnp.sum(total, axis=1, keepdims=True) + jnp.sum(e_new, axis=1, keepdims=True)
    )
    mixed = jnp.dot((e_new * inverse).astype(bf16), val_new, preferred_element_type=f32)
    for c in range(NTP // CHUNK):
        vals = kv_ref[c * CHUNK : (c + 1) * CHUNK, :, HD:].reshape(width, HD)
        w = (s_s[:, c * width : (c + 1) * width] * inverse).astype(bf16)
        mixed = mixed + jnp.dot(w, vals, preferred_element_type=f32)
    mixed = mixed.astype(bf16)
    for k, out in enumerate((o0, o1, o2, o3)):
        for h in range(2):
            row = (k * 2 + h) * NEW
            out[:, h * HD : (h + 1) * HD] = mixed[row : row + NEW]


def attend(info, pieces, kv):
    vm = pl.BlockSpec(memory_space=pltpu.VMEM)
    return pl.pallas_call(
        attend_kernel,
        in_specs=[pl.BlockSpec(memory_space=pltpu.SMEM)] + [vm] * 5,
        out_specs=[vm] * 4,
        out_shape=[jax.ShapeDtypeStruct((NEW, QC + 2 * HD), bf16)] * 4,
        scratch_shapes=[
            pltpu.VMEM((GROUP * NEW, HD), bf16),
            pltpu.VMEM((GROUP * NEW, NTP * PAGE), f32),
            pltpu.VMEM((4, NEW, HD), f32),
        ],
        cost_estimate=takes(7),
        compiler_params=pltpu.CompilerParams(vmem_limit_bytes=24 * MIB),
    )(info, *pieces, kv)


STEP = 1024
CHUNKS = ((0, 3072), (3072, 5120))


def outward_kernel(place_ref, a0, a1, a2, a3, *refs):
    wo, o0, o1, o2a, o2b, o3, rows = refs
    step = pl.program_id(0)

    @pl.when(step == 0)
    def _():
        for k, piece in enumerate((a0, a1, a2, a3)):
            at = lax.rem(place_ref[2] + k + 4 - place_ref[0], 4)
            rows[pl.ds(pl.multiple_of(at * NEW, NEW), NEW), :] = piece[...]

    part = jnp.dot(rows[...], wo[...], preferred_element_type=f32).astype(bf16)
    at = pl.ds(pl.multiple_of(step * STEP, STEP), STEP)
    o0[:, at] = part[:64]
    o1[:, at] = part[64:128]
    o2a[:, at] = part[128:160]
    o2b[:, at] = part[160:192]
    o3[:, at] = part[192:]


def outward(place, pieces, wo, first, cols):
    lead = first // STEP
    fixed = lambda n, p: (0, 0)
    shapes = [(NEW, cols), (NEW, cols), (32, cols), (32, cols), (NEW, cols)]
    return pl.pallas_call(
        outward_kernel,
        grid_spec=pltpu.PrefetchScalarGridSpec(
            num_scalar_prefetch=1,
            grid=(cols // STEP,),
            in_specs=[pl.BlockSpec((NEW, QC), fixed)] * 4
            + [pl.BlockSpec((QC, STEP), lambda n, p: (0, n + lead))],
            out_specs=[pl.BlockSpec(shape, fixed) for shape in shapes],
            scratch_shapes=[pltpu.VMEM((REQ * NEW, QC), bf16)],
        ),
        out_shape=[jax.ShapeDtypeStruct(shape, bf16) for shape in shapes],
        cost_estimate=takes(4),
        compiler_params=pltpu.CompilerParams(vmem_limit_bytes=24 * MIB),
    )(place, *pieces, wo)


def merge_kernel(first, base, got, out):
    rows, other = slice(first, first + 32), slice(32 - first, 64 - first)
    out[rows, :] = (base[rows, :].astype(f32) + got[...].astype(f32)).astype(bf16)
    out[other, :] = base[other, :]


def merge(first, base, got):
    vm = pl.BlockSpec(memory_space=pltpu.VMEM)
    return pl.pallas_call(
        functools.partial(merge_kernel, first),
        in_specs=[vm] * 2,
        out_specs=vm,
        out_shape=jax.ShapeDtypeStruct(base.shape, bf16),
        cost_estimate=takes(1),
        compiler_params=pltpu.CompilerParams(vmem_limit_bytes=16 * MIB),
    )(base, got)


def over_y_kernel(b0, right, left, out):
    total = b0[...].astype(f32) + right[...].astype(f32) + left[...].astype(f32)
    for k in range(NZ):
        out[k] = total[k * 8 : k * 8 + 8].astype(bf16)


def over_y(blocks):
    vm = pl.BlockSpec(memory_space=pltpu.VMEM)
    return pl.pallas_call(
        over_y_kernel,
        in_specs=[vm] * 3,
        out_specs=vm,
        out_shape=jax.ShapeDtypeStruct((NZ, 8, blocks[0].shape[1]), bf16),
        cost_estimate=takes(2),
        compiler_params=pltpu.CompilerParams(vmem_limit_bytes=16 * MIB),
    )(*blocks)


def finish_kernel(hidden, *refs):
    parts, out = refs[:-1], refs[-1]
    for (first, cols), part in zip(CHUNKS, parts):
        total = part[0].astype(f32)
        for k in range(1, NZ):
            total = total + part[k].astype(f32)
        at = slice(first, first + cols)
        out[:, at] = (hidden[:, at].astype(f32) + total).astype(bf16)


def finish(hidden, parts):
    vm = pl.BlockSpec(memory_space=pltpu.VMEM)
    return pl.pallas_call(
        finish_kernel,
        in_specs=[vm] * (1 + len(parts)),
        out_specs=vm,
        out_shape=jax.ShapeDtypeStruct((8, D), bf16),
        cost_estimate=takes(1),
        compiler_params=pltpu.CompilerParams(vmem_limit_bytes=16 * MIB),
    )(hidden, *parts)


def local(
    hidden, norm_gain, w_query, w_keyval, w_out, kv_pool, page_table, prefix_len, decode_place
):
    y = lax.axis_index("y")
    z = lax.axis_index("z")
    rank = y * NZ + z
    member = rank % 4
    place = jnp.stack([y, z, member]).astype(jnp.int32)
    lens = prefix_len[0]
    table = page_table[0].reshape(REQ, -1)

    xf = hidden.astype(f32)
    meansq = jnp.mean(xf * xf, axis=-1, keepdims=True)
    normed = (xf * lax.rsqrt(meansq + 1e-05) * norm_gain[0][None, :]).astype(bf16)
    half = D // 2
    toward = [t.reshape(NZ, PAGE, 2 * HD) for t in regroup(page_table[0], kv_pool[0])]
    normed, *toward = lax.optimization_barrier((normed, *toward))
    column = [toward[0]] + [shift(toward[k], "y", k) for k in range(1, NY)]

    r1, l1 = shift(normed, "z", 1), shift(normed, "z", -1)
    r2, l2 = shift(r1, "z", 1), shift(l1, "z", -1)
    r3, l3 = shift(r2, "z", 1), shift(l2, "z", -1)
    r4, l4 = shift(r3[:, :half], "z", 1), shift(l3[:, half:], "z", -1)
    mine = jnp.concatenate([normed, r1, l1, r2, l2, r3, l3, jnp.concatenate([r4, l4], 1)], 0)
    top, low = mine[:32], mine[32:]
    yr1a, yl1b = shift(top, "y", 1), shift(low, "y", -1)
    yr1b, yl1a = shift(low, "y", 1), shift(top, "y", -1)
    kv = lax.all_to_all(by_z(column), "z", split_axis=0, concat_axis=0, tiled=True)
    kv = kv.reshape(NTP, PAGE, 2 * HD)

    dims = jnp.arange(HD, dtype=jnp.int32)
    positions = (lens[:, None] + jnp.arange(NEW, dtype=jnp.int32)[None, :]).reshape(-1)
    inverse = jnp.power(rope_theta, -(dims // 2 * 2).astype(f32) / HD)
    angle = positions[:, None].astype(f32) * inverse[None, :]
    cosine, sine = jnp.cos(angle), jnp.sin(angle)
    is_key = member < 2
    tables = (cosine, sine, jnp.where(is_key, cosine, 1.0), jnp.where(is_key, sine, 0.0))
    tables = [t.reshape(REQ, NEW, HD) for t in tables]
    wkv = w_keyval[0].T
    wq = w_query[0]
    rows0 = project(place, [mine], (0,), wq, wkv, tables)
    yr1a, yl1b, rows0 = lax.optimization_barrier((yr1a, yl1b, rows0))
    yr2, yl2 = shift(yr1a, "y", 1), shift(yl1b, "y", -1)
    rows1 = project(place, [yr1a, yr1b, yl1a, yl1b], (-1, 1), wq, wkv, tables)
    projected = project(place, [yr2, yl2], (-2,), wq, wkv, tables, (rows0, rows1))

    got = [projected[0]] + [shift_quad(projected[k], k) for k in (1, 2, 3)]
    my_table = lax.dynamic_index_in_dim(table, member, 0, keepdims=False)
    owners = jnp.arange(NTP, dtype=jnp.int32)
    owners = (y - owners % NY) % NY * NZ + owners // NY
    starts = jnp.sum(
        jnp.where(my_table[None, :] // 4 == owners[:, None], jnp.arange(NTP)[None, :], 0), axis=1
    )
    my_len = jnp.sum(jnp.where(jnp.arange(REQ) == member, lens, 0))
    info = jnp.concatenate([jnp.stack([member, my_len]), starts]).astype(jnp.int32)
    attended = attend(info, got, kv)
    back = [attended[0]] + [shift_quad(attended[k], -k) for k in (1, 2, 3)]

    places = decode_place[0]
    unit_ids = jnp.arange(REQ * KVH, dtype=jnp.int32)

    def holder(slots):
        held = jnp.sum(jnp.where(places[None, :] == slots[:, None], unit_ids[None, :], 0), axis=1)
        return (held % KVH * 4 + held // KVH).astype(jnp.int32)

    held = holder((y + jnp.arange(NY, dtype=jnp.int32)) % NY * NZ + z) % NZ
    pick = jnp.where(held // 4 == z // 4, 0, 4) + (held - member) % 4
    from_y = (y - holder(rank[None])[0] // NZ) % NY

    (a0, a1, a2a, a2b, a3), (b0, b1, b2a, b2b, b3) = (
        outward(place, back, w_out[0], *CHUNKS[n]) for n in range(2)
    )
    a_right, a_left = shift(a2a, "y", 1), shift(a2b, "y", -1)
    b_right, b_left = shift(b2a, "y", 1), shift(b2b, "y", -1)
    a_right, a_left, b1, b3 = lax.optimization_barrier((a_right, a_left, b1, b3))
    a_blocks = (a0, shift(merge(0, a1, a_right), "y", 1), shift(merge(32, a3, a_left), "y", -1))
    b_to_right, b_to_left = merge(0, b1, b_right), merge(32, b3, b_left)
    units = jnp.stack([b[:, QC:] for b in back])
    b_to_right, b_to_left, units = lax.optimization_barrier((b_to_right, b_to_left, units))
    b_blocks = (b0, shift(b_to_right, "y", 1), shift(b_to_left, "y", -1))
    a_part = lax.all_to_all(over_y(a_blocks), "z", split_axis=0, concat_axis=0, tiled=True)
    units = jnp.concatenate([units, shift(units, "z", 4)], axis=0)
    *b_blocks, units = lax.optimization_barrier((*b_blocks, units))
    b_part = lax.all_to_all(over_y(b_blocks), "z", split_axis=0, concat_axis=0, tiled=True)
    chosen = [shift(units[pick[k]], "y", k) if k else units[pick[k]] for k in range(NY)]
    handed = shift(finish(hidden, (a_part, b_part)), "section", 1)
    cache = jnp.stack(chosen)[from_y]
    return handed, cache[None, None]


def solution(mesh):
    names = ("section", "y", "z")
    tp = ("y", "z")
    grid = Mesh(mesh.devices.reshape(mesh.devices.shape[0], NY, NZ), names)
    placed = (
        P(names, None),
        P("section", None),
        P("section", None, tp),
        P("section", None, tp),
        P("section", tp, None),
        P("section", tp, None, None),
        P("section", None),
        P("section", None),
        P("section", None),
    )
    return jax.shard_map(
        local,
        mesh=grid,
        in_specs=placed,
        out_specs=(P(names, None), P("section", tp, None, None)),
        check_vma=False,
    )
```

```python
import functools

import jax
import jax.numpy as jnp
from jax import lax
from jax.experimental import pallas as pl
from jax.experimental.pallas import tpu as pltpu
from jax.sharding import Mesh, PartitionSpec as P

D = 8192
KVH = 8
HD = 128
PAGE = 128
REQ = 4
NEW = 64
NY = 4
NZ = 8
NTP = 32
QC = 256
GROUP = 8

rope_theta = 500000.0
f32 = jnp.float32
bf16 = jnp.bfloat16
MIB = 1024 * 1024


def takes(us):
    return pl.CostEstimate(flops=0, bytes_accessed=int(us * 3.3e4), transcendentals=0)


def shift(value, axis, steps):
    count = lax.axis_size(axis)
    return lax.ppermute(value, axis, [(i, (i + steps) % count) for i in range(count)])


def shift_quad(value, steps):
    pairs = [(q * 4 + i, q * 4 + (i + steps) % 4) for q in range(2) for i in range(4)]
    return lax.ppermute(value, "z", pairs)


def regroup_kernel(table_ref, pool_ref, *outs):
    y = lax.axis_index("y")
    rank = y * NZ + lax.axis_index("z")
    for r in range(REQ):
        page = jnp.int32(0)
        for j in range(NTP):
            entry = table_ref[r * NTP + j]
            page = jnp.where(lax.shift_right_logical(entry, 2) == rank, entry & 3, page)
        for k, out in enumerate(outs):
            first = lax.rem(y + k, NY) * (4 * HD)
            for h in range(2):
                at = pl.multiple_of(first + h * 2 * HD, 2 * HD)
                out[h, r] = pool_ref[page, :, pl.ds(at, 2 * HD)]


def regroup(table, pool):
    vm = pl.BlockSpec(memory_space=pltpu.VMEM)
    return pl.pallas_call(
        regroup_kernel,
        in_specs=[pl.BlockSpec(memory_space=pltpu.SMEM), vm],
        out_specs=[vm] * NY,
        out_shape=[jax.ShapeDtypeStruct((2, REQ, PAGE, 2 * HD), bf16)] * NY,
        cost_estimate=takes(2),
        compiler_params=pltpu.CompilerParams(vmem_limit_bytes=16 * MIB),
    )(table, pool)


def by_z_kernel(c0, c1, c2, c3, out):
    for z in range(NZ):
        for k, column in enumerate((c0, c1, c2, c3)):
            out[z, k] = column[z]


def by_z(column):
    vm = pl.BlockSpec(memory_space=pltpu.VMEM)
    return pl.pallas_call(
        by_z_kernel,
        in_specs=[vm] * NY,
        out_specs=vm,
        out_shape=jax.ShapeDtypeStruct((NZ, NY, PAGE, 2 * HD), bf16),
        cost_estimate=takes(2),
        compiler_params=pltpu.CompilerParams(vmem_limit_bytes=16 * MIB),
    )(*column)


def pack_kernel(*refs):
    pieces, out = refs[:-1], refs[-1]
    for first in range(0, D, KC):
        cols = slice(first, first + KC)
        rows = [p[:, cols].astype(f32) for p in pieces[:3]]
        if len(pieces) == 4:
            rows.append(pieces[3][:, cols].astype(f32))
        else:
            rest = pieces[3] if first < D // 2 else pieces[4]
            rows.append(rest[:, first % (D // 2) : first % (D // 2) + KC].astype(f32))
        out[:, cols] = jnp.concatenate(rows, axis=0).astype(bf16)


def pack(*pieces):
    vm = pl.BlockSpec(memory_space=pltpu.VMEM)
    return pl.pallas_call(
        pack_kernel,
        in_specs=[vm] * len(pieces),
        out_specs=vm,
        out_shape=jax.ShapeDtypeStruct((32, D), bf16),
        cost_estimate=takes(1),
        compiler_params=pltpu.CompilerParams(vmem_limit_bytes=56 * MIB),
    )(*pieces)


Z_ORDER = (0, -1, 1, -2, 2, -3, 3, -4)
KC = 2048


def project_kernel(ks, split, last, *refs):
    place_ref, refs = refs[0], refs[1:]
    pieces, refs = refs[: len(split)], refs[len(split) :]
    wq, wkv, cosine, sine, cosine_kv, sine_kv = refs[:6]
    before, refs = refs[6 : 6 + 2 * last], refs[6 + 2 * last :]
    outs, (acc, turned, wide, *ready) = refs[: -3 - last], refs[-3 - last :]
    step = pl.program_id(0)
    mine = lax.rem(place_ref[2], 2) * 64
    wide[pl.ds(pl.multiple_of(mine, 64), 64), :] = wkv[...]
    wide[pl.ds(pl.multiple_of(64 - mine, 64), 64), :] = jnp.zeros((64, KC), bf16)
    rows = jnp.concatenate([piece[...] for piece in pieces], axis=0)
    part_q = jnp.dot(rows, wq[...], preferred_element_type=f32)
    part_kv = lax.dot_general(
        rows, wide[...], (((1,), (1,)), ((), ())), preferred_element_type=f32
    )

    @pl.when(step == 0)
    def _():
        acc[:, :QC] = part_q
        acc[:, QC:] = part_kv

    @pl.when(step > 0)
    def _():
        acc[:, :QC] += part_q
        acc[:, QC:] += part_kv

    @pl.when(step == pl.num_programs(0) - 1)
    def _():
        even = lax.broadcasted_iota(jnp.int32, (NEW, HD), 1) % 2 == 0
        for n, k in enumerate(ks):
            request = lax.rem(place_ref[0] + (k + NY), NY)
            for j in range(NZ):
                zj = lax.rem(place_ref[1] + (Z_ORDER[j] + NZ), NZ)
                turned[pl.ds(pl.multiple_of(zj * 8, 8), 8), :] = acc[
                    n * NEW + j * 8 : n * NEW + j * 8 + 8, :
                ]
            for c in range(3):
                v = turned[:, c * HD : (c + 1) * HD]
                cs, sn = (cosine, sine) if c < 2 else (cosine_kv, sine_kv)
                other = jnp.where(even, -pltpu.roll(v, HD - 1, 1), pltpu.roll(v, 1, 1))
                done = (v * cs[request] + other * sn[request]).astype(bf16)
                if last:
                    ready[0][request, :, c * HD : (c + 1) * HD] = done
                else:
                    outs[0][n, :, c * HD : (c + 1) * HD] = done
        if last:
            for n, k in enumerate((0, -1, 1)):
                request = lax.rem(place_ref[0] + (k + NY), NY)
                ready[0][request] = before[0][0] if n == 0 else before[1][n - 1]
            for k, out in enumerate(outs):
                out[...] = ready[0][lax.rem(place_ref[2] + k, REQ)]


def project(place, pieces, ks, wq, wkv, tables, before=()):
    split = [p.shape[0] for p in pieces]
    last = 1 if before else 0
    rows = sum(split)
    whole = pl.BlockSpec((REQ, NEW, HD), lambda k, p: (0, 0, 0))
    width = QC + HD
    if last:
        out_specs = [pl.BlockSpec((NEW, width), lambda k, p: (0, 0))] * REQ
        out_shape = [jax.ShapeDtypeStruct((NEW, width), bf16)] * REQ
    else:
        out_specs = [pl.BlockSpec((len(ks), NEW, width), lambda k, p: (0, 0, 0))]
        out_shape = [jax.ShapeDtypeStruct((len(ks), NEW, width), bf16)]
    out = pl.pallas_call(
        functools.partial(project_kernel, ks, split, last),
        grid_spec=pltpu.PrefetchScalarGridSpec(
            num_scalar_prefetch=1,
            grid=(D // KC,),
            in_specs=[pl.BlockSpec((r, KC), lambda k, p: (0, k)) for r in split]
            + [
                pl.BlockSpec((KC, QC), lambda k, p: (k, 0)),
                pl.BlockSpec((64, KC), lambda k, p: (0, k)),
            ]
            + [whole] * 4
            + [pl.BlockSpec(b.shape, lambda k, p: (0, 0, 0)) for b in before],
            out_specs=out_specs,
            scratch_shapes=[
                pltpu.VMEM((rows, width), f32),
                pltpu.VMEM((NEW, width), f32),
                pltpu.VMEM((HD, KC), bf16),
            ]
            + [pltpu.VMEM((REQ, NEW, width), bf16)] * last,
        ),
        out_shape=out_shape,
        cost_estimate=takes(300),
        compiler_params=pltpu.CompilerParams(vmem_limit_bytes=16 * MIB),
    )(place, *pieces, wq, wkv, *tables, *before)
    return out if last else out[0]


CHUNK = 4


def attend_kernel(info_ref, p0, p1, p2, p3, kv_ref, o0, o1, o2, o3, q_s, s_s, fresh):
    pieces = (p0, p1, p2, p3)
    member = info_ref[0]
    length = info_ref[1]
    for k in range(4):
        for h in range(2):
            row = (k * 2 + h) * NEW
            q_s[row : row + NEW, :] = pieces[k][:, h * HD : (h + 1) * HD]
        fresh[k] = pieces[k][:, QC:].astype(f32)
    key_new = (fresh[lax.rem(member, 4)] + fresh[lax.rem(member + 3, 4)]).astype(bf16)
    val_new = (fresh[lax.rem(member + 2, 4)] + fresh[lax.rem(member + 1, 4)]).astype(bf16)
    for out in (o0, o1, o2, o3):
        out[:, QC : QC + HD] = key_new
        out[:, QC + HD :] = val_new
    q = q_s[...]
    rows = GROUP * NEW
    nt = (((1,), (1,)), ((), ()))
    s_new = lax.dot_general(q, key_new, nt, preferred_element_type=f32)
    token = lax.broadcasted_iota(jnp.int32, (rows, NEW), 0) % NEW
    s_new = jnp.where(lax.broadcasted_iota(jnp.int32, (rows, NEW), 1) <= token, s_new, -1e30)
    top = jnp.full((rows, HD), -1e30, f32)
    lane = lax.broadcasted_iota(jnp.int32, (1, HD), 1)
    width = CHUNK * PAGE
    for c in range(NTP // CHUNK):
        keys = kv_ref[c * CHUNK : (c + 1) * CHUNK, :, :HD].reshape(width, HD)
        s = lax.dot_general(q, keys, nt, preferred_element_type=f32)
        for o in range(CHUNK):
            start = info_ref[2 + c * CHUNK + o] * PAGE
            part = jnp.where(lane < length - start, s[:, o * PAGE : (o + 1) * PAGE], -1e30)
            s_s[:, c * width + o * PAGE : c * width + (o + 1) * PAGE] = part
            top = jnp.maximum(top, part)
    m = jnp.maximum(
        jnp.max(top, axis=1, keepdims=True), jnp.max(s_new, axis=1, keepdims=True)
    )
    factor = HD ** (-0.5) * 1.4426950408889634
    e_new = jnp.exp2((s_new - m) * factor)
    total = jnp.zeros((rows, HD), f32)
    for c in range(NTP):
        e = jnp.exp2((s_s[:, c * PAGE : (c + 1) * PAGE] - m) * factor)
        s_s[:, c * PAGE : (c + 1) * PAGE] = e
        total = total + e
    inverse = 1.0 / (
        jnp.sum(total, axis=1, keepdims=True) + jnp.sum(e_new, axis=1, keepdims=True)
    )
    mixed = jnp.dot((e_new * inverse).astype(bf16), val_new, preferred_element_type=f32)
    for c in range(NTP // CHUNK):
        vals = kv_ref[c * CHUNK : (c + 1) * CHUNK, :, HD:].reshape(width, HD)
        w = (s_s[:, c * width : (c + 1) * width] * inverse).astype(bf16)
        mixed = mixed + jnp.dot(w, vals, preferred_element_type=f32)
    mixed = mixed.astype(bf16)
    for k, out in enumerate((o0, o1, o2, o3)):
        for h in range(2):
            row = (k * 2 + h) * NEW
            out[:, h * HD : (h + 1) * HD] = mixed[row : row + NEW]


def attend(info, pieces, kv):
    vm = pl.BlockSpec(memory_space=pltpu.VMEM)
    return pl.pallas_call(
        attend_kernel,
        in_specs=[pl.BlockSpec(memory_space=pltpu.SMEM)] + [vm] * 5,
        out_specs=[vm] * 4,
        out_shape=[jax.ShapeDtypeStruct((NEW, QC + 2 * HD), bf16)] * 4,
        scratch_shapes=[
            pltpu.VMEM((GROUP * NEW, HD), bf16),
            pltpu.VMEM((GROUP * NEW, NTP * PAGE), f32),
            pltpu.VMEM((4, NEW, HD), f32),
        ],
        cost_estimate=takes(7),
        compiler_params=pltpu.CompilerParams(vmem_limit_bytes=24 * MIB),
    )(info, *pieces, kv)


FIRST = 6144
LAST = D - FIRST


def outward_kernel(first, cols, place_ref, a0, a1, a2, a3, wo, *refs):
    *outs, rows = refs
    for k, piece in enumerate((a0, a1, a2, a3)):
        at = lax.rem(place_ref[2] + k + 4 - place_ref[0], 4)
        rows[pl.ds(pl.multiple_of(at * NEW, NEW), NEW), :] = piece[:, :QC]
    step = cols // (4 if cols > 4096 else 2)
    for begin in range(0, cols, step):
        at = slice(begin, begin + step)
        part = jnp.dot(
            rows[...], wo[:, first + begin : first + begin + step], preferred_element_type=f32
        )
        if len(outs) == 1:
            for k in range(NZ):
                block = [part[j * NEW + k * 8 : j * NEW + k * 8 + 8] for j in range(NY)]
                outs[0][k, :, at] = jnp.concatenate(block, axis=0).astype(bf16)
        else:
            top = 0
            for out in outs:
                out[:, at] = part[top : top + out.shape[0]].astype(bf16)
                top += out.shape[0]


def outward(place, pieces, wo, first, cols, shapes):
    vm = pl.BlockSpec(memory_space=pltpu.VMEM)
    return pl.pallas_call(
        functools.partial(outward_kernel, first, cols),
        in_specs=[pl.BlockSpec(memory_space=pltpu.SMEM)] + [vm] * 5,
        out_specs=[vm] * len(shapes),
        out_shape=[jax.ShapeDtypeStruct(s, bf16) for s in shapes],
        scratch_shapes=[pltpu.VMEM((REQ * NEW, QC), bf16)],
        cost_estimate=takes(4),
        compiler_params=pltpu.CompilerParams(vmem_limit_bytes=24 * MIB),
    )(place, *pieces, wo)


def merge_kernel(first, base, got, out):
    rows, other = slice(first, first + 32), slice(32 - first, 64 - first)
    out[rows, :] = (base[rows, :].astype(f32) + got[...].astype(f32)).astype(bf16)
    out[other, :] = base[other, :]


def merge(first, base, got):
    vm = pl.BlockSpec(memory_space=pltpu.VMEM)
    return pl.pallas_call(
        functools.partial(merge_kernel, first),
        in_specs=[vm] * 2,
        out_specs=vm,
        out_shape=jax.ShapeDtypeStruct(base.shape, bf16),
        cost_estimate=takes(1),
        compiler_params=pltpu.CompilerParams(vmem_limit_bytes=16 * MIB),
    )(base, got)


def over_y_kernel(first, *refs):
    rest, out = refs[:-1], refs[-1]
    total = first[...].astype(f32)
    for block in rest:
        total = total + block[...].astype(f32)
    for k in range(NZ):
        out[k] = total[k * 8 : k * 8 + 8].astype(bf16)


def over_y(blocks):
    vm = pl.BlockSpec(memory_space=pltpu.VMEM)
    return pl.pallas_call(
        over_y_kernel,
        in_specs=[vm] * len(blocks),
        out_specs=vm,
        out_shape=jax.ShapeDtypeStruct((NZ, 8, blocks[0].shape[1]), bf16),
        cost_estimate=takes(2),
        compiler_params=pltpu.CompilerParams(vmem_limit_bytes=16 * MIB),
    )(*blocks)


def choose_kernel(pick_ref, units, *outs):
    for k, out in enumerate(outs):
        out[...] = units[pick_ref[k]]


def choose(pick, units):
    vm = pl.BlockSpec(memory_space=pltpu.VMEM)
    count = pick.shape[0]
    return pl.pallas_call(
        choose_kernel,
        in_specs=[pl.BlockSpec(memory_space=pltpu.SMEM), vm],
        out_specs=[vm] * count,
        out_shape=[jax.ShapeDtypeStruct(units.shape[1:], bf16)] * count,
        cost_estimate=takes(1),
        compiler_params=pltpu.CompilerParams(vmem_limit_bytes=16 * MIB),
    )(pick, units)


def over_z_kernel(got, *outs):
    total = got[0].astype(f32)
    for k in range(1, NZ):
        total = total + got[k].astype(f32)
    for j, out in enumerate(outs):
        out[...] = total[j * 8 : j * 8 + 8].astype(bf16)


def over_z(got):
    vm = pl.BlockSpec(memory_space=pltpu.VMEM)
    return pl.pallas_call(
        over_z_kernel,
        in_specs=[vm],
        out_specs=[vm] * NY,
        out_shape=[jax.ShapeDtypeStruct((8, LAST), bf16)] * NY,
        cost_estimate=takes(1),
        compiler_params=pltpu.CompilerParams(vmem_limit_bytes=16 * MIB),
    )(got)


def finish_kernel(hidden, part, l0, l1, l2, l3, out):
    total = part[0].astype(f32)
    for k in range(1, NZ):
        total = total + part[k].astype(f32)
    out[:, :FIRST] = (hidden[:, :FIRST].astype(f32) + total).astype(bf16)
    total = (l0[...].astype(f32) + l1[...].astype(f32)) + (l2[...].astype(f32) + l3[...].astype(f32))
    out[:, FIRST:] = (hidden[:, FIRST:].astype(f32) + total).astype(bf16)


def finish(hidden, part, late):
    vm = pl.BlockSpec(memory_space=pltpu.VMEM)
    return pl.pallas_call(
        finish_kernel,
        in_specs=[vm] * 6,
        out_specs=vm,
        out_shape=jax.ShapeDtypeStruct((8, D), bf16),
        cost_estimate=takes(1),
        compiler_params=pltpu.CompilerParams(vmem_limit_bytes=16 * MIB),
    )(hidden, part, *late)


def local(
    hidden, norm_gain, w_query, w_keyval, w_out, kv_pool, page_table, prefix_len, decode_place
):
    y = lax.axis_index("y")
    z = lax.axis_index("z")
    rank = y * NZ + z
    member = rank % 4
    place = jnp.stack([y, z, member]).astype(jnp.int32)
    lens = prefix_len[0]
    table = page_table[0].reshape(REQ, -1)

    xf = hidden.astype(f32)
    meansq = jnp.mean(xf * xf, axis=-1, keepdims=True)
    normed = (xf * lax.rsqrt(meansq + 1e-05) * norm_gain[0][None, :]).astype(bf16)
    toward = [t.reshape(NZ, PAGE, 2 * HD) for t in regroup(page_table[0], kv_pool[0])]
    normed, *toward = lax.optimization_barrier((normed, *toward))
    column = [toward[0]] + [shift(toward[k], "y", k) for k in range(1, NY)]

    half = D // 2
    r1, l1 = shift(normed, "z", 1), shift(normed, "z", -1)
    r2, l2 = shift(r1, "z", 1), shift(l1, "z", -1)
    r3, l3 = shift(r2, "z", 1), shift(l2, "z", -1)
    r4, l4 = shift(r3[:, :half], "z", 1), shift(l3[:, half:], "z", -1)
    *column, r4, l4 = lax.optimization_barrier((*column, r4, l4))
    kv = lax.all_to_all(by_z(column), "z", split_axis=0, concat_axis=0, tiled=True)
    top, low = pack(normed, r1, l1, r2), pack(l2, r3, l3, r4, l4)
    yr1a, yl1b = shift(top, "y", 1), shift(low, "y", -1)
    yr1b, yl1a = shift(low, "y", 1), shift(top, "y", -1)
    kv = kv.reshape(NTP, PAGE, 2 * HD)

    dims = jnp.arange(HD, dtype=jnp.int32)
    positions = (lens[:, None] + jnp.arange(NEW, dtype=jnp.int32)[None, :]).reshape(-1)
    inverse = jnp.power(rope_theta, -(dims // 2 * 2).astype(f32) / HD)
    angle = positions[:, None].astype(f32) * inverse[None, :]
    cosine, sine = jnp.cos(angle), jnp.sin(angle)
    is_key = member < 2
    tables = (cosine, sine, jnp.where(is_key, cosine, 1.0), jnp.where(is_key, sine, 0.0))
    tables = [t.reshape(REQ, NEW, HD) for t in tables]
    wkv = w_keyval[0].T
    wq = w_query[0]
    rows0 = project(place, [top, low], (0,), wq, wkv, tables)
    yr2, yl2 = shift(yr1a, "y", 1), shift(yl1b, "y", -1)
    rows1 = project(place, [yr1a, yr1b, yl1a, yl1b], (-1, 1), wq, wkv, tables)
    projected = project(place, [yr2, yl2], (-2,), wq, wkv, tables, (rows0, rows1))

    got = [projected[0]] + [shift_quad(projected[k], k) for k in (1, 2, 3)]
    my_table = lax.dynamic_index_in_dim(table, member, 0, keepdims=False)
    owners = jnp.arange(NTP, dtype=jnp.int32)
    owners = (y - owners % NY) % NY * NZ + owners // NY
    starts = jnp.sum(
        jnp.where(my_table[None, :] // 4 == owners[:, None], jnp.arange(NTP)[None, :], 0), axis=1
    )
    my_len = jnp.sum(jnp.where(jnp.arange(REQ) == member, lens, 0))
    info = jnp.concatenate([jnp.stack([member, my_len]), starts]).astype(jnp.int32)
    attended = attend(info, got, kv)
    back = [attended[0]] + [shift_quad(attended[k], -k) for k in (1, 2, 3)]

    places = decode_place[0]
    unit_ids = jnp.arange(REQ * KVH, dtype=jnp.int32)

    def holder(slots):
        held = jnp.sum(jnp.where(places[None, :] == slots[:, None], unit_ids[None, :], 0), axis=1)
        return (held % KVH * 4 + held // KVH).astype(jnp.int32)

    held = holder((y + jnp.arange(NY, dtype=jnp.int32)) % NY * NZ + z) % NZ
    pick = jnp.where(held // 4 == z // 4, 0, 4) + (held - member) % 4
    from_y = (y - holder(rank[None])[0] // NZ) % NY

    units = jnp.stack([b[:, QC:] for b in back])
    wo = w_out[0]
    shapes = [(n, FIRST) for n in (64, 64, 32, 32, 64)]
    o0, o1, o2a, o2b, o3 = outward(place, back, wo, 0, FIRST, shapes)
    o2a, o2b, *back = lax.optimization_barrier((o2a, o2b, *back))
    (late,) = outward(place, back, wo, FIRST, LAST, [(NZ, 32, LAST)])
    right, left = shift(o2a, "y", 1), shift(o2b, "y", -1)
    others = shift(units, "z", 4)
    right, left, others, late = lax.optimization_barrier((right, left, others, late))
    blocks = (o0, shift(merge(0, o1, right), "y", 1), shift(merge(32, o3, left), "y", -1))
    late = over_z(lax.all_to_all(late, "z", split_axis=0, concat_axis=0, tiled=True))
    chosen = choose(pick, jnp.concatenate([units, others], axis=0))
    chosen = [chosen[0]] + [shift(chosen[k], "y", k) for k in (1, 2, 3)]
    *blocks, chosen, late = lax.optimization_barrier((*blocks, chosen, late))
    part = lax.all_to_all(over_y(blocks), "z", split_axis=0, concat_axis=0, tiled=True)
    late = [late[0]] + [shift(late[k], "y", k) for k in (1, 2, 3)]
    handed = shift(finish(hidden, part, late), "section", 1)
    (cache,) = choose(from_y[None], jnp.stack(chosen))
    return handed, cache[None, None]


def solution(mesh):
    names = ("section", "y", "z")
    tp = ("y", "z")
    grid = Mesh(mesh.devices.reshape(mesh.devices.shape[0], NY, NZ), names)
    placed = (
        P(names, None),
        P("section", None),
        P("section", None, tp),
        P("section", None, tp),
        P("section", tp, None),
        P("section", tp, None, None),
        P("section", None),
        P("section", None),
        P("section", None),
    )
    return jax.shard_map(
        local,
        mesh=grid,
        in_specs=placed,
        out_specs=(P(names, None), P("section", tp, None, None)),
        check_vma=False,
    )
```

```python
import functools

import jax
import jax.numpy as jnp
from jax import lax
from jax.experimental import pallas as pl
from jax.experimental.pallas import tpu as pltpu
from jax.sharding import Mesh, PartitionSpec as P

D = 8192
KVH = 8
HD = 128
PAGE = 128
REQ = 4
NEW = 64
NY = 4
NZ = 8
NTP = 32
QC = 256
GROUP = 8

rope_theta = 500000.0
f32 = jnp.float32
bf16 = jnp.bfloat16
MIB = 1024 * 1024


def takes(us):
    return pl.CostEstimate(flops=0, bytes_accessed=int(us * 3.3e4), transcendentals=0)


def shift(value, axis, steps):
    count = lax.axis_size(axis)
    return lax.ppermute(value, axis, [(i, (i + steps) % count) for i in range(count)])


def shift_quad(value, steps):
    pairs = [(q * 4 + i, q * 4 + (i + steps) % 4) for q in range(2) for i in range(4)]
    return lax.ppermute(value, "z", pairs)


def after_kernel(*refs):
    pass


def after(value, *others):
    anywhere = pl.BlockSpec(memory_space=pl.ANY)
    return pl.pallas_call(
        after_kernel,
        in_specs=[anywhere] * (1 + len(others)),
        out_specs=anywhere,
        out_shape=jax.ShapeDtypeStruct(value.shape, value.dtype),
        input_output_aliases={0: 0},
    )(value, *others)


def regroup_kernel(table_ref, pool_ref, *outs):
    y = lax.axis_index("y")
    rank = y * NZ + lax.axis_index("z")
    for r in range(REQ):
        page = jnp.int32(0)
        for j in range(NTP):
            entry = table_ref[r * NTP + j]
            page = jnp.where(lax.shift_right_logical(entry, 2) == rank, entry & 3, page)
        for k, out in enumerate(outs):
            first = lax.rem(y + k, NY) * (4 * HD)
            for h in range(2):
                at = pl.multiple_of(first + h * 2 * HD, 2 * HD)
                out[h, r] = pool_ref[page, :, pl.ds(at, 2 * HD)]


def regroup(table, pool):
    vm = pl.BlockSpec(memory_space=pltpu.VMEM)
    return pl.pallas_call(
        regroup_kernel,
        in_specs=[pl.BlockSpec(memory_space=pltpu.SMEM), vm],
        out_specs=[vm] * NY,
        out_shape=[jax.ShapeDtypeStruct((2, REQ, PAGE, 2 * HD), bf16)] * NY,
        cost_estimate=takes(2),
        compiler_params=pltpu.CompilerParams(vmem_limit_bytes=16 * MIB),
    )(table, pool)


def by_z_kernel(c0, c1, c2, c3, out):
    for z in range(NZ):
        for k, column in enumerate((c0, c1, c2, c3)):
            out[z, k] = column[z]


def by_z(column):
    vm = pl.BlockSpec(memory_space=pltpu.VMEM)
    return pl.pallas_call(
        by_z_kernel,
        in_specs=[vm] * NY,
        out_specs=vm,
        out_shape=jax.ShapeDtypeStruct((NZ, NY, PAGE, 2 * HD), bf16),
        cost_estimate=takes(2),
        compiler_params=pltpu.CompilerParams(vmem_limit_bytes=16 * MIB),
    )(*column)


def pack_kernel(*refs):
    pieces, out = refs[:-1], refs[-1]
    for first in range(0, D, KC):
        cols = slice(first, first + KC)
        rows = [p[:, cols].astype(f32) for p in pieces[:3]]
        if len(pieces) == 4:
            rows.append(pieces[3][:, cols].astype(f32))
        else:
            rest = pieces[3] if first < D // 2 else pieces[4]
            rows.append(rest[:, first % (D // 2) : first % (D // 2) + KC].astype(f32))
        out[:, cols] = jnp.concatenate(rows, axis=0).astype(bf16)


def pack(*pieces):
    vm = pl.BlockSpec(memory_space=pltpu.VMEM)
    return pl.pallas_call(
        pack_kernel,
        in_specs=[vm] * len(pieces),
        out_specs=vm,
        out_shape=jax.ShapeDtypeStruct((32, D), bf16),
        cost_estimate=takes(1),
        compiler_params=pltpu.CompilerParams(vmem_limit_bytes=56 * MIB),
    )(*pieces)


Z_ORDER = (0, -1, 1, -2, 2, -3, 3, -4)
KC = 2048


def project_kernel(ks, split, last, *refs):
    place_ref, refs = refs[0], refs[1:]
    pieces, refs = refs[: len(split)], refs[len(split) :]
    wq, wkv, cosine, sine, cosine_kv, sine_kv = refs[:6]
    before, refs = refs[6 : 6 + 2 * last], refs[6 + 2 * last :]
    outs, (acc, turned, wide, *ready) = refs[: -3 - last], refs[-3 - last :]
    step = pl.program_id(0)
    mine = lax.rem(place_ref[2], 2) * 64
    wide[pl.ds(pl.multiple_of(mine, 64), 64), :] = wkv[...]
    wide[pl.ds(pl.multiple_of(64 - mine, 64), 64), :] = jnp.zeros((64, KC), bf16)
    rows = jnp.concatenate([piece[...] for piece in pieces], axis=0)
    part_q = jnp.dot(rows, wq[...], preferred_element_type=f32)
    part_kv = lax.dot_general(
        rows, wide[...], (((1,), (1,)), ((), ())), preferred_element_type=f32
    )

    @pl.when(step == 0)
    def _():
        acc[:, :QC] = part_q
        acc[:, QC:] = part_kv

    @pl.when(step > 0)
    def _():
        acc[:, :QC] += part_q
        acc[:, QC:] += part_kv

    @pl.when(step == pl.num_programs(0) - 1)
    def _():
        even = lax.broadcasted_iota(jnp.int32, (NEW, HD), 1) % 2 == 0
        for n, k in enumerate(ks):
            request = lax.rem(place_ref[0] + (k + NY), NY)
            for j in range(NZ):
                zj = lax.rem(place_ref[1] + (Z_ORDER[j] + NZ), NZ)
                turned[pl.ds(pl.multiple_of(zj * 8, 8), 8), :] = acc[
                    n * NEW + j * 8 : n * NEW + j * 8 + 8, :
                ]
            for c in range(3):
                v = turned[:, c * HD : (c + 1) * HD]
                cs, sn = (cosine, sine) if c < 2 else (cosine_kv, sine_kv)
                other = jnp.where(even, -pltpu.roll(v, HD - 1, 1), pltpu.roll(v, 1, 1))
                done = (v * cs[request] + other * sn[request]).astype(bf16)
                if last:
                    ready[0][request, :, c * HD : (c + 1) * HD] = done
                else:
                    outs[0][n, :, c * HD : (c + 1) * HD] = done
        if last:
            for n, k in enumerate((0, -1, 1)):
                request = lax.rem(place_ref[0] + (k + NY), NY)
                ready[0][request] = before[0][0] if n == 0 else before[1][n - 1]
            for k, out in enumerate(outs):
                out[...] = ready[0][lax.rem(place_ref[2] + k, REQ)]


def project(place, pieces, ks, wq, wkv, tables, before=()):
    split = [p.shape[0] for p in pieces]
    last = 1 if before else 0
    rows = sum(split)
    whole = pl.BlockSpec((REQ, NEW, HD), lambda k, p: (0, 0, 0))
    width = QC + HD
    if last:
        out_specs = [pl.BlockSpec((NEW, width), lambda k, p: (0, 0))] * REQ
        out_shape = [jax.ShapeDtypeStruct((NEW, width), bf16)] * REQ
    else:
        out_specs = [pl.BlockSpec((len(ks), NEW, width), lambda k, p: (0, 0, 0))]
        out_shape = [jax.ShapeDtypeStruct((len(ks), NEW, width), bf16)]
    out = pl.pallas_call(
        functools.partial(project_kernel, ks, split, last),
        grid_spec=pltpu.PrefetchScalarGridSpec(
            num_scalar_prefetch=1,
            grid=(D // KC,),
            in_specs=[pl.BlockSpec((r, KC), lambda k, p: (0, k)) for r in split]
            + [
                pl.BlockSpec((KC, QC), lambda k, p: (k, 0)),
                pl.BlockSpec((64, KC), lambda k, p: (0, k)),
            ]
            + [whole] * 4
            + [pl.BlockSpec(b.shape, lambda k, p: (0, 0, 0)) for b in before],
            out_specs=out_specs,
            scratch_shapes=[
                pltpu.VMEM((rows, width), f32),
                pltpu.VMEM((NEW, width), f32),
                pltpu.VMEM((HD, KC), bf16),
            ]
            + [pltpu.VMEM((REQ, NEW, width), bf16)] * last,
        ),
        out_shape=out_shape,
        cost_estimate=takes(300),
        compiler_params=pltpu.CompilerParams(vmem_limit_bytes=16 * MIB),
    )(place, *pieces, wq, wkv, *tables, *before)
    return out if last else out[0]


CHUNK = 4


def attend_kernel(info_ref, p0, p1, p2, p3, kv_ref, o0, o1, o2, o3, q_s, s_s, fresh):
    pieces = (p0, p1, p2, p3)
    member = info_ref[0]
    length = info_ref[1]
    for k in range(4):
        for h in range(2):
            row = (k * 2 + h) * NEW
            q_s[row : row + NEW, :] = pieces[k][:, h * HD : (h + 1) * HD]
        fresh[k] = pieces[k][:, QC:].astype(f32)
    key_new = (fresh[lax.rem(member, 4)] + fresh[lax.rem(member + 3, 4)]).astype(bf16)
    val_new = (fresh[lax.rem(member + 2, 4)] + fresh[lax.rem(member + 1, 4)]).astype(bf16)
    for out in (o0, o1, o2, o3):
        out[:, QC : QC + HD] = key_new
        out[:, QC + HD :] = val_new
    q = q_s[...]
    rows = GROUP * NEW
    nt = (((1,), (1,)), ((), ()))
    s_new = lax.dot_general(q, key_new, nt, preferred_element_type=f32)
    token = lax.broadcasted_iota(jnp.int32, (rows, NEW), 0) % NEW
    s_new = jnp.where(lax.broadcasted_iota(jnp.int32, (rows, NEW), 1) <= token, s_new, -1e30)
    top = jnp.full((rows, HD), -1e30, f32)
    lane = lax.broadcasted_iota(jnp.int32, (1, HD), 1)
    width = CHUNK * PAGE
    for c in range(NTP // CHUNK):
        keys = kv_ref[c * CHUNK : (c + 1) * CHUNK, :, :HD].reshape(width, HD)
        s = lax.dot_general(q, keys, nt, preferred_element_type=f32)
        for o in range(CHUNK):
            start = info_ref[2 + c * CHUNK + o] * PAGE
            part = jnp.where(lane < length - start, s[:, o * PAGE : (o + 1) * PAGE], -1e30)
            s_s[:, c * width + o * PAGE : c * width + (o + 1) * PAGE] = part
            top = jnp.maximum(top, part)
    m = jnp.maximum(
        jnp.max(top, axis=1, keepdims=True), jnp.max(s_new, axis=1, keepdims=True)
    )
    factor = HD ** (-0.5) * 1.4426950408889634
    e_new = jnp.exp2((s_new - m) * factor)
    total = jnp.zeros((rows, HD), f32)
    for c in range(NTP):
        e = jnp.exp2((s_s[:, c * PAGE : (c + 1) * PAGE] - m) * factor)
        s_s[:, c * PAGE : (c + 1) * PAGE] = e
        total = total + e
    inverse = 1.0 / (
        jnp.sum(total, axis=1, keepdims=True) + jnp.sum(e_new, axis=1, keepdims=True)
    )
    mixed = jnp.dot((e_new * inverse).astype(bf16), val_new, preferred_element_type=f32)
    for c in range(NTP // CHUNK):
        vals = kv_ref[c * CHUNK : (c + 1) * CHUNK, :, HD:].reshape(width, HD)
        w = (s_s[:, c * width : (c + 1) * width] * inverse).astype(bf16)
        mixed = mixed + jnp.dot(w, vals, preferred_element_type=f32)
    mixed = mixed.astype(bf16)
    for k, out in enumerate((o0, o1, o2, o3)):
        for h in range(2):
            row = (k * 2 + h) * NEW
            out[:, h * HD : (h + 1) * HD] = mixed[row : row + NEW]


def attend(info, pieces, kv):
    vm = pl.BlockSpec(memory_space=pltpu.VMEM)
    return pl.pallas_call(
        attend_kernel,
        in_specs=[pl.BlockSpec(memory_space=pltpu.SMEM)] + [vm] * 5,
        out_specs=[vm] * 4,
        out_shape=[jax.ShapeDtypeStruct((NEW, QC + 2 * HD), bf16)] * 4,
        scratch_shapes=[
            pltpu.VMEM((GROUP * NEW, HD), bf16),
            pltpu.VMEM((GROUP * NEW, NTP * PAGE), f32),
            pltpu.VMEM((4, NEW, HD), f32),
        ],
        cost_estimate=takes(7),
        compiler_params=pltpu.CompilerParams(vmem_limit_bytes=24 * MIB),
    )(info, *pieces, kv)


FIRST = 6144
LAST = D - FIRST


def outward_kernel(first, cols, place_ref, a0, a1, a2, a3, wo, *refs):
    *outs, rows = refs
    for k, piece in enumerate((a0, a1, a2, a3)):
        at = lax.rem(place_ref[2] + k + 4 - place_ref[0], 4)
        rows[pl.ds(pl.multiple_of(at * NEW, NEW), NEW), :] = piece[:, :QC]
    step = cols // (4 if cols > 4096 else 2)
    for begin in range(0, cols, step):
        at = slice(begin, begin + step)
        part = jnp.dot(
            rows[...], wo[:, first + begin : first + begin + step], preferred_element_type=f32
        )
        if len(outs) == 1:
            for k in range(NZ):
                block = [part[j * NEW + k * 8 : j * NEW + k * 8 + 8] for j in range(NY)]
                outs[0][k, :, at] = jnp.concatenate(block, axis=0).astype(bf16)
        else:
            top = 0
            for out in outs:
                out[:, at] = part[top : top + out.shape[0]].astype(bf16)
                top += out.shape[0]


def outward(place, pieces, wo, first, cols, shapes):
    vm = pl.BlockSpec(memory_space=pltpu.VMEM)
    return pl.pallas_call(
        functools.partial(outward_kernel, first, cols),
        in_specs=[pl.BlockSpec(memory_space=pltpu.SMEM)] + [vm] * 5,
        out_specs=[vm] * len(shapes),
        out_shape=[jax.ShapeDtypeStruct(s, bf16) for s in shapes],
        scratch_shapes=[pltpu.VMEM((REQ * NEW, QC), bf16)],
        cost_estimate=takes(4),
        compiler_params=pltpu.CompilerParams(vmem_limit_bytes=24 * MIB),
    )(place, *pieces, wo)


def merge_kernel(first, base, got, out):
    rows, other = slice(first, first + 32), slice(32 - first, 64 - first)
    out[rows, :] = (base[rows, :].astype(f32) + got[...].astype(f32)).astype(bf16)
    out[other, :] = base[other, :]


def merge(first, base, got):
    vm = pl.BlockSpec(memory_space=pltpu.VMEM)
    return pl.pallas_call(
        functools.partial(merge_kernel, first),
        in_specs=[vm] * 2,
        out_specs=vm,
        out_shape=jax.ShapeDtypeStruct(base.shape, bf16),
        cost_estimate=takes(1),
        compiler_params=pltpu.CompilerParams(vmem_limit_bytes=16 * MIB),
    )(base, got)


def over_y_kernel(first, *refs):
    rest, out = refs[:-1], refs[-1]
    total = first[...].astype(f32)
    for block in rest:
        total = total + block[...].astype(f32)
    for k in range(NZ):
        out[k] = total[k * 8 : k * 8 + 8].astype(bf16)


def over_y(blocks):
    vm = pl.BlockSpec(memory_space=pltpu.VMEM)
    return pl.pallas_call(
        over_y_kernel,
        in_specs=[vm] * len(blocks),
        out_specs=vm,
        out_shape=jax.ShapeDtypeStruct((NZ, 8, blocks[0].shape[1]), bf16),
        cost_estimate=takes(2),
        compiler_params=pltpu.CompilerParams(vmem_limit_bytes=16 * MIB),
    )(*blocks)


def choose_kernel(pick_ref, here, there, *outs):
    for k, out in enumerate(outs):

        @pl.when(pick_ref[k] < 4)
        def _(k=k, out=out):
            out[...] = here[pick_ref[k] & 3]

        @pl.when(pick_ref[k] >= 4)
        def _(k=k, out=out):
            out[...] = there[pick_ref[k] & 3]


def choose(pick, here, there):
    vm = pl.BlockSpec(memory_space=pltpu.VMEM)
    count = pick.shape[0]
    return pl.pallas_call(
        choose_kernel,
        in_specs=[pl.BlockSpec(memory_space=pltpu.SMEM), vm, vm],
        out_specs=[vm] * count,
        out_shape=[jax.ShapeDtypeStruct(here.shape[1:], bf16)] * count,
        cost_estimate=takes(1),
        compiler_params=pltpu.CompilerParams(vmem_limit_bytes=16 * MIB),
    )(pick, here, there)


def over_z_kernel(got, *outs):
    total = got[0].astype(f32)
    for k in range(1, NZ):
        total = total + got[k].astype(f32)
    for j, out in enumerate(outs):
        out[...] = total[j * 8 : j * 8 + 8].astype(bf16)


def over_z(got):
    vm = pl.BlockSpec(memory_space=pltpu.VMEM)
    return pl.pallas_call(
        over_z_kernel,
        in_specs=[vm],
        out_specs=[vm] * NY,
        out_shape=[jax.ShapeDtypeStruct((8, LAST), bf16)] * NY,
        cost_estimate=takes(1),
        compiler_params=pltpu.CompilerParams(vmem_limit_bytes=16 * MIB),
    )(got)


def finish_kernel(hidden, part, l0, l1, l2, l3, out):
    total = part[0].astype(f32)
    for k in range(1, NZ):
        total = total + part[k].astype(f32)
    out[:, :FIRST] = (hidden[:, :FIRST].astype(f32) + total).astype(bf16)
    total = (l0[...].astype(f32) + l1[...].astype(f32)) + (l2[...].astype(f32) + l3[...].astype(f32))
    out[:, FIRST:] = (hidden[:, FIRST:].astype(f32) + total).astype(bf16)


def finish(hidden, part, late):
    vm = pl.BlockSpec(memory_space=pltpu.VMEM)
    return pl.pallas_call(
        finish_kernel,
        in_specs=[vm] * 6,
        out_specs=vm,
        out_shape=jax.ShapeDtypeStruct((8, D), bf16),
        cost_estimate=takes(1),
        compiler_params=pltpu.CompilerParams(vmem_limit_bytes=16 * MIB),
    )(hidden, part, *late)


def local(
    hidden, norm_gain, w_query, w_keyval, w_out, kv_pool, page_table, prefix_len, decode_place
):
    y = lax.axis_index("y")
    z = lax.axis_index("z")
    rank = y * NZ + z
    member = rank % 4
    place = jnp.stack([y, z, member]).astype(jnp.int32)
    lens = prefix_len[0]
    table = page_table[0].reshape(REQ, -1)

    xf = hidden.astype(f32)
    meansq = jnp.mean(xf * xf, axis=-1, keepdims=True)
    normed = (xf * lax.rsqrt(meansq + 1e-05) * norm_gain[0][None, :]).astype(bf16)
    toward = [t.reshape(NZ, PAGE, 2 * HD) for t in regroup(page_table[0], kv_pool[0])]
    normed, *toward = lax.optimization_barrier((normed, *toward))
    column = [toward[0]] + [shift(toward[k], "y", k) for k in range(1, NY)]

    half = D // 2
    r1, l1 = shift(normed, "z", 1), shift(normed, "z", -1)
    r2, l2 = shift(r1, "z", 1), shift(l1, "z", -1)
    r3, l3 = shift(r2, "z", 1), shift(l2, "z", -1)
    r4, l4 = shift(r3[:, :half], "z", 1), shift(l3[:, half:], "z", -1)
    *column, r4, l4 = lax.optimization_barrier((*column, r4, l4))
    kv = lax.all_to_all(by_z(column), "z", split_axis=0, concat_axis=0, tiled=True)
    top, low = pack(normed, r1, l1, r2), pack(l2, r3, l3, r4, l4)
    yr1a, yl1b = shift(top, "y", 1), shift(low, "y", -1)
    yr1b, yl1a = shift(low, "y", 1), shift(top, "y", -1)
    kv = kv.reshape(NTP, PAGE, 2 * HD)

    dims = jnp.arange(HD, dtype=jnp.int32)
    positions = (lens[:, None] + jnp.arange(NEW, dtype=jnp.int32)[None, :]).reshape(-1)
    inverse = jnp.power(rope_theta, -(dims // 2 * 2).astype(f32) / HD)
    angle = positions[:, None].astype(f32) * inverse[None, :]
    cosine, sine = jnp.cos(angle), jnp.sin(angle)
    is_key = member < 2
    tables = (cosine, sine, jnp.where(is_key, cosine, 1.0), jnp.where(is_key, sine, 0.0))
    tables = [t.reshape(REQ, NEW, HD) for t in tables]
    wkv = w_keyval[0].T
    wq = w_query[0]
    rows0 = project(place, [top, low], (0,), wq, wkv, tables)
    yr2, yl2 = shift(yr1a, "y", 1), shift(yl1b, "y", -1)
    rows1 = project(place, [yr1a, yr1b, yl1a, yl1b], (-1, 1), wq, wkv, tables)
    projected = project(place, [yr2, yl2], (-2,), wq, wkv, tables, (rows0, rows1))

    got = [projected[0]] + [shift_quad(projected[k], k) for k in (1, 2, 3)]
    my_table = lax.dynamic_index_in_dim(table, member, 0, keepdims=False)
    owners = jnp.arange(NTP, dtype=jnp.int32)
    owners = (y - owners % NY) % NY * NZ + owners // NY
    starts = jnp.sum(
        jnp.where(my_table[None, :] // 4 == owners[:, None], jnp.arange(NTP)[None, :], 0), axis=1
    )
    my_len = jnp.sum(jnp.where(jnp.arange(REQ) == member, lens, 0))
    info = jnp.concatenate([jnp.stack([member, my_len]), starts]).astype(jnp.int32)
    attended = attend(info, got, kv)
    back = [attended[0]] + [shift_quad(attended[k], -k) for k in (1, 2, 3)]

    places = decode_place[0]
    unit_ids = jnp.arange(REQ * KVH, dtype=jnp.int32)

    def holder(slots):
        held = jnp.sum(jnp.where(places[None, :] == slots[:, None], unit_ids[None, :], 0), axis=1)
        return (held % KVH * 4 + held // KVH).astype(jnp.int32)

    held = holder((y + jnp.arange(NY, dtype=jnp.int32)) % NY * NZ + z) % NZ
    pick = jnp.where(held // 4 == z // 4, 0, 4) + (held - member) % 4
    from_y = (y - holder(rank[None])[0] // NZ) % NY

    units = jnp.stack([b[:, QC:] for b in back])
    wo = w_out[0]
    shapes = [(n, FIRST) for n in (64, 64, 32, 32, 64)]
    o0, o1, o2a, o2b, o3 = outward(place, back, wo, 0, FIRST, shapes)
    o2a, o2b, *back = lax.optimization_barrier((o2a, o2b, *back))
    (late,) = outward(place, back, wo, FIRST, LAST, [(NZ, 32, LAST)])
    right, left = shift(o2a, "y", 1), shift(o2b, "y", -1)
    others = shift(units, "z", 4)
    late = after(late, right, left, others)
    blocks = (o0, shift(merge(0, o1, right), "y", 1), shift(merge(32, o3, left), "y", -1))
    late = over_z(lax.all_to_all(late, "z", split_axis=0, concat_axis=0, tiled=True))
    chosen = choose(pick, units, others)
    chosen = [chosen[0]] + [shift(chosen[k], "y", k) for k in (1, 2, 3)]
    blocks = (after(o0, late[0], *chosen[1:]), *blocks[1:])
    part = lax.all_to_all(over_y(blocks), "z", split_axis=0, concat_axis=0, tiled=True)
    late = [late[0]] + [shift(late[k], "y", k) for k in (1, 2, 3)]
    handed = shift(finish(hidden, part, late), "section", 1)
    chosen = jnp.stack(chosen)
    (cache,) = choose(from_y[None], chosen, chosen)
    return handed, cache[None, None]


def solution(mesh):
    names = ("section", "y", "z")
    tp = ("y", "z")
    grid = Mesh(mesh.devices.reshape(mesh.devices.shape[0], NY, NZ), names)
    placed = (
        P(names, None),
        P("section", None),
        P("section", None, tp),
        P("section", None, tp),
        P("section", tp, None),
        P("section", tp, None, None),
        P("section", None),
        P("section", None),
        P("section", None),
    )
    return jax.shard_map(
        local,
        mesh=grid,
        in_specs=placed,
        out_specs=(P(names, None), P("section", tp, None, None)),
        check_vma=False,
    )
```
